128 devices in a mesh: dp: 128 (over z, y, x, core).
Axes of the slice: x: 4, y: 4, z: 4, core: 2. Of those that a mesh axis runs over, the one named last changes fastest.
Arguments:
- tokens: bfloat16 [16384, 768], P('dp'), may hold values from -6 to 6
- cotangent: bfloat16 [16384, 768], P('dp'), may hold values from -6 to 6
- lengths: int32 [128, 4], P('dp'), may hold values from 1 to 80, 128 in all within a row
- gains: float32 [2, 768], P(None, 'dp'), may hold values from 0.5 to 1.5
- gain_moment: float32 [2, 768], P(None, 'dp'), may hold values from -384 to 384
- qkv_weight: float32 [3, 768, 768], P(None, 'dp'), may hold values from -0.21875 to 0.21875
- out_weight: float32 [768, 768], P('dp'), may hold values from -0.625 to 0.625
- inner_weight: float32 [2, 768, 3072], P(None, 'dp'), may hold values from -0.21875 to 0.21875
- down_weight: float32 [3072, 768], P('dp'), may hold values from -0.109375 to 0.109375
- qkv_moment: float32 [3, 768, 768], P(None, 'dp'), may hold values from -224 to 224
- out_moment: float32 [768, 768], P('dp'), may hold values from -224 to 224
- inner_moment: float32 [2, 768, 3072], P(None, 'dp'), may hold values from -224 to 224
- down_moment: float32 [3072, 768], P('dp'), may hold values from -224 to 224
Outputs:
- block_output: bfloat16 [16384, 768], P('dp')
- input_grad: float32 [16384, 768], P('dp')
- gain_grad: float32 [2, 768], P(None, 'dp')
- gain_moment_new: float32 [2, 768], P(None, 'dp')
- gains_new: float32 [2, 768], P(None, 'dp')
- qkv_grad: float32 [3, 768, 768], P(None, 'dp')
- out_grad: float32 [768, 768], P('dp')
- inner_grad: float32 [2, 768, 3072], P(None, 'dp')
- down_grad: float32 [3072, 768], P('dp')
- qkv_new: float32 [3, 768, 768], P(None, 'dp')
- out_new: float32 [768, 768], P('dp')
- inner_new: float32 [2, 768, 3072], P(None, 'dp')
- down_new: float32 [3072, 768], P('dp')
- qkv_moment_new: float32 [3, 768, 768], P(None, 'dp')
- out_moment_new: float32 [768, 768], P('dp')
- inner_moment_new: float32 [2, 768, 3072], P(None, 'dp')
- down_moment_new: float32 [3072, 768], P('dp')
The draws below stay inside these ranges and needn't reach their ends.
Inputs may be any that keep to these rules, and one draw needn't show every extreme that they name: Each row holds the lengths of the 4 sequences that fill one pack of 128 tokens in order; in every row the longest is exactly 80.
All inputs are finite; a program needn't handle non-finite values.
Results may differ from the reference program's by a relative error of at most 0.012.
The reference program's roundings to bfloat16 on the way count: a program that leaves them out, or rounds other values in their place, can miss the bound.
Values may be sent and summed in bfloat16 or wider, within the bound.
No kernel may reach another device: no remote copies, remote signals or barrier semaphores. Data moves between devices by JAX's collectives and lax.ppermute only.
A program may use at most 192 MiB of HBM per device.

```python
import math
import jax
import jax.numpy as jnp
import numpy as np
from jax import lax

D = 768
FF = 3072
HEAD = 64
TOK_DEV = 128
SLOTS = 4
NS_ITERS = 2
PACKS = 128
TOKENS = 16384


def block_scale(rng, extent, cuts, smallest, largest):
    factor_of = 1.0
    for axis_at, blocks in cuts:
        steps = jax.random.uniform(jax.random.fold_in(jax.random.fold_in(rng, 6), axis_at), (blocks,), jnp.float32, smallest / len(cuts), largest / len(cuts))
        factor_of = factor_of * jnp.repeat(jnp.exp(steps), extent[axis_at] // blocks).reshape((-1,) + (1,) * (len(extent) - 1 - axis_at))
    return factor_of


def profile(number_of, total, limit, lean):
    loads = [(1 << 20) // math.isqrt(grade ** lean) + 1 for grade in range(2, number_of + 1)]
    surplus, counts = total - limit - (number_of - 1), [1] * (number_of - 1)
    while surplus > 0:
        movable = [i for i in range(number_of - 1) if counts[i] < limit]
        mass, left = sum([loads[i] for i in movable]), surplus
        for i in movable:
            addition = min(limit - counts[i], max(1, left * loads[i] // mass), surplus)
            counts[i] = counts[i] + addition
            surplus = surplus - addition
    return np.array([limit] + counts)


def ragged(own_key, count, total, bound, skew):
    if count == 2:
        one = jax.random.randint(own_key, (), max(1, total - bound), min(bound, total - 1) + 1)
        return jnp.stack([one, total - one])
    tallies = jnp.asarray(profile(count, total, bound, skew), jnp.int32)
    couples = (count - 1) // 2
    donor, sink = tallies[1:1 + 2 * couples:2], tallies[2:2 + 2 * couples:2]
    room = jnp.minimum(donor - 1, bound - sink)
    passed = jax.random.randint(jax.random.fold_in(own_key, 1), (couples,), 0, 1 << 20) % (room + 1)
    tallies = tallies.at[1:1 + 2 * couples:2].set(donor - passed).at[2:2 + 2 * couples:2].set(sink + passed)
    return tallies[jax.random.permutation(jax.random.fold_in(own_key, 2), count)]


def normal_values(stream_key, extent, deviation, bound, cuts=(), kind=jnp.bfloat16):
    values = deviation * jax.random.normal(stream_key, extent, jnp.float32)
    if cuts:
        values = values * block_scale(stream_key, extent, cuts, -0.22, 0.18)
    return jnp.clip(values, -bound, bound).astype(kind)


def setup_inputs(seed: int = 0) -> dict:
    seeds = jax.random.split(jax.random.key(seed), 14)
    tokens = normal_values(seeds[0], (TOKENS, D), 1.0, 6.0, ((0, 128),))
    cotangent = normal_values(seeds[1], (TOKENS, D), 1.0, 6.0, ((0, 128),))
    lengths = jax.vmap(lambda own: ragged(own, SLOTS, TOK_DEV, 5 * TOK_DEV // 8, 2))(jax.random.split(seeds[2], PACKS)).reshape((PACKS, SLOTS)).astype(jnp.int32)
    gains = jnp.clip(1.0 + 0.1 * jax.random.normal(seeds[3], (2, D), jnp.float32), 0.5, 1.5)
    gain_moment = normal_values(seeds[4], (2, D), (0.5 * TOKENS ** 0.5), 384.0, ((1, 128),), jnp.float32)
    qkv_weight = normal_values(seeds[5], (3, D, D), D ** -0.5, 0.21875, ((1, 128),), jnp.float32)
    out_weight = normal_values(seeds[6], (D, D), (D // 9) ** -0.5, 0.625, ((0, 128),), jnp.float32)
    inner_weight = normal_values(seeds[7], (2, D, FF), D ** -0.5, 0.21875, ((1, 128),), jnp.float32)
    down_weight = normal_values(seeds[8], (FF, D), FF ** -0.5, 0.109375, ((0, 128),), jnp.float32)
    qkv_moment = normal_values(seeds[9], (3, D, D), (0.3 * TOKENS ** 0.5), 224.0, ((1, 128),), jnp.float32)
    out_moment = normal_values(seeds[10], (D, D), (0.3 * TOKENS ** 0.5), 224.0, ((0, 128),), jnp.float32)
    inner_moment = normal_values(seeds[11], (2, D, FF), (0.3 * TOKENS ** 0.5), 224.0, ((1, 128),), jnp.float32)
    down_moment = normal_values(seeds[12], (FF, D), (0.3 * TOKENS ** 0.5), 224.0, ((0, 128),), jnp.float32)
    return {"tokens": tokens, "cotangent": cotangent, "lengths": lengths, "gains": gains, "gain_moment": gain_moment, "qkv_weight": qkv_weight, "out_weight": out_weight, "inner_weight": inner_weight, "down_weight": down_weight, "qkv_moment": qkv_moment, "out_moment": out_moment, "inner_moment": inner_moment, "down_moment": down_moment}


EPSILON = 1e-06
ROPE_BASE = 10000.0
MOMENTUM = 0.95
GAIN_MOMENTUM = 0.9
MUON_RATE = 0.3
GAIN_RATE = 0.001
WEIGHT_DECAY = 0.1
POLY_LINEAR = 3.4445
POLY_CUBIC = -4.775
POLY_QUINTIC = 2.0315

@jax.custom_vjp
def low(v):
    return lax.optimization_barrier(v.astype(jnp.bfloat16)).astype(jnp.float32)

@jax.custom_vjp
def low_back(v):
    return v

def low_keep(v):
    return (low(v), None)

def low_pass(kept, grad):
    return (grad,)

def back_keep(v):
    return (v, None)

def back_low(kept, grad):
    return (low(grad),)
low.defvjp(low_keep, low_pass)
low_back.defvjp(back_keep, back_low)

def segment_table(lengths, count):
    ends = jnp.cumsum(lengths, dtype=jnp.int32)
    places = jnp.arange(count, dtype=jnp.int32)
    segment = lax.optimization_barrier(jnp.sum((places[:, None] >= ends[None, :]).astype(jnp.int32), axis=1, dtype=jnp.int32))
    starts = ends - lengths
    slots = jnp.arange(lengths.shape[0], dtype=jnp.int32)
    first = lax.optimization_barrier(jnp.sum(jnp.where(segment[:, None] == slots[None, :], starts[None, :], 0), axis=1, dtype=jnp.int32))
    return (segment, places - first)

def rotate(values, position, sign):
    half = values.shape[-1] // 2
    freq = ROPE_BASE ** (-jnp.arange(half, dtype=jnp.float32) / half)
    angle = position.astype(jnp.float32)[:, None] * freq[None, :]
    cosine = jnp.cos(angle)[:, None, :]
    sine = sign * jnp.sin(angle)[:, None, :]
    first = values[..., :half]
    second = values[..., half:]
    return jnp.concatenate([first * cosine - second * sine, second * cosine + first * sine], axis=-1)

def norm_scale(values):
    return lax.rsqrt(lax.optimization_barrier(jnp.mean(values * values, axis=-1, keepdims=True)) + EPSILON)

def product(left, right):
    return jnp.dot(left, right, precision=lax.Precision.HIGHEST, preferred_element_type=jnp.float32)

def block_forward(tokens, segment, position, gains_b, qkv_b, out_b, inner_b, down_b):
    count = tokens.shape[0]
    places = jnp.arange(count, dtype=jnp.int32)
    normed = low(tokens * norm_scale(tokens) * gains_b[0])
    query = low_back(product(normed, qkv_b[0])).reshape(count, D // HEAD, HEAD)
    keys = low_back(product(normed, qkv_b[1])).reshape(count, D // HEAD, HEAD)
    values = low(low_back(product(normed, qkv_b[2]))).reshape(count, D // HEAD, HEAD)
    query = low(rotate(query, position, 1.0))
    keys = low(rotate(keys, position, 1.0))
    dots = low_back(jnp.einsum('qhd,khd->hqk', query, keys, precision=lax.Precision.HIGHEST)) * HEAD ** (-0.5)
    allowed = (segment[:, None] == segment[None, :]) & (places[None, :] <= places[:, None])
    dots = jnp.where(allowed[None], dots, -1e+30)
    top = lax.optimization_barrier(jnp.max(dots, axis=-1, keepdims=True))
    weights = jnp.exp(dots - top)
    probs = low(weights / lax.optimization_barrier(jnp.sum(weights, axis=-1, keepdims=True)))
    mixed = low(low_back(jnp.einsum('hqk,khd->qhd', probs, values, precision=lax.Precision.HIGHEST))).reshape(count, D)
    branch = low_back(product(mixed, out_b))
    middle = tokens + branch
    normed_two = low(middle * norm_scale(middle) * gains_b[1])
    gate = low_back(product(normed_two, inner_b[0]))
    upward = low_back(product(normed_two, inner_b[1]))
    hidden = low(jax.nn.silu(gate) * upward)
    return middle + low_back(product(hidden, down_b))

def orthogonalize(moment):
    flip = moment.shape[0] > moment.shape[1]
    matrix = moment.T if flip else moment
    matrix = matrix / (jnp.sqrt(jnp.sum(matrix * matrix)) + 1e-07)
    for turn in range(NS_ITERS):
        square = jnp.dot(matrix, matrix.T, precision=lax.Precision.HIGHEST)
        poly = POLY_CUBIC * square + POLY_QUINTIC * jnp.dot(square, square, precision=lax.Precision.HIGHEST)
        matrix = POLY_LINEAR * matrix + jnp.dot(poly, matrix, precision=lax.Precision.HIGHEST)
    return matrix.T if flip else matrix

def muon_step(weight, moment_new):
    rows, cols = weight.shape
    update = orthogonalize(moment_new) * (0.2 * math.sqrt(max(rows, cols)))
    return weight * (1.0 - MUON_RATE * WEIGHT_DECAY) - MUON_RATE * update

def reference(tokens, cotangent, lengths, gains, gain_moment, qkv_weight, out_weight, inner_weight, down_weight, qkv_moment, out_moment, inner_moment, down_moment):
    segment, position = jax.vmap(lambda row: segment_table(row, TOK_DEV))(lengths)
    group = math.gcd(PACKS, max(1, 4096 // TOK_DEV))
    batches = PACKS // group

    def forward(inputs, gains_f, qkv_f, out_f, inner_f, down_f):
        gains_b = low(gains_f)
        qkv_b = low(qkv_f)
        out_b = low(out_f)
        inner_b = low(inner_f)
        down_b = low(down_f)

        def run_group(pieces):
            block_tokens, block_segment, block_position = pieces
            return jax.vmap(lambda first, second, third: block_forward(first, second, third, gains_b, qkv_b, out_b, inner_b, down_b))(block_tokens, block_segment, block_position)
        result = lax.map(jax.checkpoint(run_group), (inputs.reshape(batches, group, TOK_DEV, D), segment.reshape(batches, group, TOK_DEV), position.reshape(batches, group, TOK_DEV)))
        return result.reshape(TOKENS, D)
    outcome, pullback = jax.vjp(forward, tokens.astype(jnp.float32), gains, qkv_weight, out_weight, inner_weight, down_weight)
    input_grad, gain_grad, qkv_grad, out_grad, inner_grad, down_grad = pullback(cotangent.astype(jnp.float32))
    qkv_moment_new = MOMENTUM * qkv_moment + qkv_grad
    out_moment_new = MOMENTUM * out_moment + out_grad
    inner_moment_new = MOMENTUM * inner_moment + inner_grad
    down_moment_new = MOMENTUM * down_moment + down_grad
    qkv_new = jnp.stack([muon_step(qkv_weight[index], qkv_moment_new[index]) for index in range(3)])
    out_new = muon_step(out_weight, out_moment_new)
    inner_new = jnp.stack([muon_step(inner_weight[index], inner_moment_new[index]) for index in range(2)])
    down_new = muon_step(down_weight, down_moment_new)
    gain_moment_new = GAIN_MOMENTUM * gain_moment + gain_grad
    gains_new = gains - GAIN_RATE * gain_moment_new
    return (outcome.astype(jnp.bfloat16), input_grad, gain_grad, gain_moment_new, gains_new, qkv_grad, out_grad, inner_grad, down_grad, qkv_new, out_new, inner_new, down_new, qkv_moment_new, out_moment_new, inner_moment_new, down_moment_new)
```

```python
import math

import jax
import jax.numpy as jnp
import numpy as np
from jax import lax
from jax.sharding import Mesh
from jax.sharding import PartitionSpec as P

HEAD = 64
HALF = 384
WIDTH = 768
PACK = 128
EPSILON = 1e-06
ROPE_BASE = 10000.0
MOMENTUM = 0.95
GAIN_MOMENTUM = 0.9
MUON_RATE = 0.3
GAIN_RATE = 0.001
WEIGHT_DECAY = 0.1
POLY_LINEAR = 3.4445
POLY_CUBIC = -4.775
POLY_QUINTIC = 2.0315

AXES = ("z", "y", "x", "c")
SWAP = [(0, 1), (1, 0)]
BF = jnp.bfloat16
F32 = jnp.float32


def mm(left, right):
    return jnp.dot(left, right, preferred_element_type=F32)


def mm_nt(left, right):
    return lax.dot_general(left, right, (((1,), (1,)), ((), ())), preferred_element_type=F32)


def mm_tn(left, right):
    return lax.dot_general(left, right, (((0,), (0,)), ((), ())), preferred_element_type=F32)


def swap_core(value):
    return lax.ppermute(value, "c", SWAP)


def by_core(core, own, other):
    return jnp.where(core == 0, jnp.stack([own, other]), jnp.stack([other, own]))


def shift(axis, step):
    return [(i, (i + step) % 4) for i in range(4)]


def scatter_sum(chunks, axis):
    me = lax.axis_index(axis)
    total = lax.dynamic_index_in_dim(chunks, me, 0, keepdims=False).astype(F32)
    for step in (1, 3, 2):
        piece = lax.dynamic_index_in_dim(chunks, (me + step) % 4, 0, keepdims=False)
        total = total + lax.ppermute(piece, axis, shift(axis, step)).astype(F32)
    return total


def gather_four(value, axis):
    me = lax.axis_index(axis)
    full = jnp.zeros((4,) + value.shape, value.dtype)
    full = lax.dynamic_update_index_in_dim(full, value, me, 0)
    for step in (1, 3, 2):
        got = lax.ppermute(value, axis, shift(axis, step))
        full = lax.dynamic_update_index_in_dim(full, got, (me + 4 - step) % 4, 0)
    return full


def gather_xc(value, core):
    line = gather_four(value, "x")
    both = by_core(core, line, swap_core(line))
    return jnp.moveaxis(both, 0, 1).reshape((8 * value.shape[0],) + value.shape[1:])


def exchange(value, axis):
    return lax.all_to_all(value, axis, split_axis=0, concat_axis=0, tiled=True)


def one_hot(order):
    table = np.zeros((len(order), len(order)), np.float32)
    table[np.asarray(order), np.arange(len(order))] = 1.0
    return jnp.asarray(table, BF)


def norm_order():
    grid = np.arange(WIDTH).reshape(4, 4, 4, 2, 6)
    return grid.transpose(2, 3, 1, 0, 4).reshape(-1)


def out_order():
    grid = np.arange(HALF).reshape(2, 4, 4, 2, 6)
    return grid.transpose(2, 3, 1, 0, 4).reshape(-1)


def down_order():
    grid = np.arange(HALF).reshape(2, 4, 2, 24)
    return grid.transpose(1, 2, 0, 3).reshape(-1)


def segment_table(lengths, count):
    ends = jnp.cumsum(lengths, dtype=jnp.int32)
    places = jnp.arange(count, dtype=jnp.int32)
    segment = jnp.sum((places[:, None] >= ends[None, :]).astype(jnp.int32), axis=1, dtype=jnp.int32)
    starts = ends - lengths
    slots = jnp.arange(lengths.shape[0], dtype=jnp.int32)
    first = jnp.sum(
        jnp.where(segment[:, None] == slots[None, :], starts[None, :], 0), axis=1, dtype=jnp.int32
    )
    return (segment, places - first)


def rotate(values, cosine, sine):
    half = values.shape[-1] // 2
    first = values[..., :half]
    second = values[..., half:]
    return jnp.concatenate(
        [first * cosine - second * sine, second * cosine + first * sine], axis=-1
    )


def norm_scale(values):
    return lax.rsqrt(jnp.mean(values * values, axis=-1, keepdims=True) + EPSILON)


def norm_backward(values, scale, gain, grad):
    scaled = grad * gain
    return scale * scaled - values * (scale * scale * scale) * jnp.mean(
        scaled * values, axis=-1, keepdims=True
    )


def to_units(qkv, out, inner, down):
    first = jnp.concatenate([qkv, out[None]])
    wide = inner.reshape(2, 6, 4, WIDTH).transpose(0, 2, 1, 3)
    pieces = jnp.concatenate([first[None], wide, down.reshape(1, 4, 6, WIDTH)])
    got = exchange(pieces, "z")
    turned = jnp.where(lax.axis_index("z") == 3, got, got.transpose(1, 0, 2, 3))
    return exchange(turned, "y").reshape(96, WIDTH)


def to_owners(rows):
    got = exchange(rows.reshape(4, 4, 6, WIDTH), "y")
    turned = jnp.where(lax.axis_index("z") == 3, got, got.transpose(1, 0, 2, 3))
    back = exchange(turned, "z")
    inner = back[1:3].transpose(0, 2, 1, 3).reshape(2, 6, 4 * WIDTH)
    return back[0, :3], back[0, 3], inner, back[3].reshape(24, WIDTH)


def per_device(
    tokens,
    cotangent,
    lengths,
    gains,
    gain_moment,
    qkv_weight,
    out_weight,
    inner_weight,
    down_weight,
    qkv_moment,
    out_moment,
    inner_moment,
    down_moment,
):
    z, y, x, core = (lax.axis_index(name) for name in AXES)
    first = jnp.concatenate([qkv_weight, out_weight[None]]).astype(BF)
    first = first.reshape(4, 6, 2, HALF).transpose(0, 2, 1, 3)
    wide = inner_weight.astype(BF).reshape(2, 6, 4, 2, HALF).transpose(0, 2, 3, 1, 4)
    blocks = jnp.stack([first, wide[0], wide[1]], axis=2).reshape(8, 3, 6, HALF)
    blocks = exchange(blocks, ("x", "c")).transpose(1, 0, 2, 3).reshape(144, HALF)
    down_piece = down_weight.astype(BF).reshape(24, 2, HALF).transpose(1, 0, 2).reshape(48, HALF)
    gain_piece = jnp.pad(gains.astype(BF), ((0, 14), (0, HALF - 6)))
    piece = jnp.concatenate([blocks, down_piece, gain_piece])
    whole = lax.all_gather(piece, AXES, axis=0, tiled=False)
    tokens2 = by_core(core, tokens, swap_core(tokens)).reshape(2 * PACK, WIDTH)
    cot2 = by_core(core, cotangent, swap_core(cotangent)).reshape(2 * PACK, WIDTH)
    lengths2 = by_core(core, lengths[0], swap_core(lengths[0].astype(F32)).astype(jnp.int32))
    moment_rows = to_units(qkv_moment, out_moment, inner_moment, down_moment)
    segment, position = jax.vmap(lambda row: segment_table(row, PACK))(lengths2)
    freq = ROPE_BASE ** (-jnp.arange(HEAD // 2, dtype=F32) / (HEAD // 2))
    angle = position.astype(F32)[:, :, None] * freq
    cosine = jnp.cos(angle)[:, :, None, :]
    sine = jnp.sin(angle)[:, :, None, :]
    places = jnp.arange(PACK, dtype=jnp.int32)
    allowed = (segment[:, :, None] == segment[:, None, :]) & (places[None, :] <= places[:, None])
    allowed = allowed[:, None]
    inputs = tokens2.astype(F32)
    scale_one = norm_scale(inputs)

    grid = whole.reshape(16, 4, 2, 208, HALF)
    gains_full = (
        whole[:, 192:194, :6].transpose(1, 0, 2).reshape(2, WIDTH).astype(F32)
    )
    mine = lax.dynamic_index_in_dim(grid, core, 2, keepdims=False)
    qkv_c = mine[:, :3, 0:48].transpose(1, 0, 2, 3).reshape(3, WIDTH, HALF)
    out_full = grid[:, 3, :, 0:48].transpose(0, 2, 1, 3).reshape(WIDTH, WIDTH)
    gate_c = mine[:, :, 48:96].transpose(0, 2, 1, 3).reshape(WIDTH, 4 * HALF)
    up_c = mine[:, :, 96:144].transpose(0, 2, 1, 3).reshape(WIDTH, 4 * HALF)
    down_c = lax.dynamic_index_in_dim(
        whole.reshape(4, 2, 16, 208, HALF), core, 1, keepdims=False
    )[:, :, 144:192]
    down_c = down_c.reshape(4, 16, 2, 24, HALF).transpose(0, 1, 3, 2, 4).reshape(4 * HALF, WIDTH)

    normed = (inputs * scale_one * gains_full[0]).astype(BF)
    heads = HALF // HEAD
    by_head = (2, PACK, heads, HEAD)
    query = rotate(mm(normed, qkv_c[0]).reshape(by_head), cosine, sine).astype(BF)
    keys = rotate(mm(normed, qkv_c[1]).reshape(by_head), cosine, sine).astype(BF)
    values = mm(normed, qkv_c[2]).astype(BF).reshape(by_head)
    dots = jnp.einsum("pqhd,pkhd->phqk", query, keys, preferred_element_type=F32) * HEAD**-0.5
    dots = jnp.where(allowed, dots, -1e30)
    top = jnp.max(dots, axis=-1, keepdims=True)
    weights = jnp.exp(dots - top)
    total = jnp.sum(weights, axis=-1, keepdims=True)
    probs = weights / total
    probs_low = probs.astype(BF)
    mixed_c = jnp.einsum("phqk,pkhd->pqhd", probs_low, values, preferred_element_type=F32)
    mixed_c = mixed_c.astype(BF).reshape(2 * PACK, HALF)
    both = by_core(core, mixed_c, swap_core(mixed_c))
    mixed = jnp.concatenate([both[0], both[1]], axis=1)
    middle = inputs + mm(mixed, out_full)
    scale_two = norm_scale(middle)
    normed_two = (middle * scale_two * gains_full[1]).astype(BF)
    gate = mm(normed_two, gate_c)
    upward = mm(normed_two, up_c)
    sigma = jax.nn.sigmoid(gate)
    activated = gate * sigma
    hidden = (activated * upward).astype(BF)

    def own_pack(value):
        return lax.dynamic_slice_in_dim(value, core * PACK, PACK, 0)

    def other_pack(value):
        return lax.dynamic_slice_in_dim(value, (1 - core) * PACK, PACK, 0)

    down_order_hot = one_hot(down_order())
    hidden_turned = mm(hidden.reshape(-1, HALF), down_order_hot).astype(BF).reshape(2 * PACK, 4 * HALF)
    down_grad = mm_tn(hidden_turned, cot2).astype(BF)
    down_chunks = (
        down_grad.reshape(4, 8, 48, 2, HALF).transpose(0, 1, 3, 2, 4).reshape(4, 4, 192, HALF)
    )
    hidden_grad = mm_nt(cot2, down_c)
    gate_grad = (hidden_grad * upward * (sigma * (1.0 + gate * (1.0 - sigma)))).astype(BF)
    up_grad = (hidden_grad * activated).astype(BF)
    turn = one_hot(norm_order())
    two_turned = mm(normed_two, turn).astype(BF)

    def column_chunks(rows, grad):
        part = mm_tn(rows, grad).astype(BF)
        blocks_of = part.shape[1] // HALF
        return part.reshape(4, 192, blocks_of, HALF).transpose(2, 0, 1, 3)

    gate_chunks = column_chunks(two_turned, gate_grad)
    up_chunks = column_chunks(two_turned, up_grad)
    two_part = mm_nt(gate_grad, gate_c) + mm_nt(up_grad, up_c)
    normed_two_grad = two_part + swap_core(two_part)
    middle_grad = cot2.astype(F32) + norm_backward(
        middle, scale_two, gains_full[1], normed_two_grad
    )
    branch_grad = middle_grad.astype(BF)
    down_part = mm(hidden, down_c)
    block_output = (
        own_pack(middle) + own_pack(down_part) + swap_core(other_pack(down_part))
    ).astype(BF)

    def rows_first(chunks):
        return scatter_sum(jnp.swapaxes(chunks, 0, 1), "x").astype(BF)

    def units_first(chunks):
        return scatter_sum(chunks, "y").astype(BF)

    down_rows = rows_first(down_chunks)
    up_rows = units_first(up_chunks)
    gate_rows = rows_first(gate_chunks)

    out_turned = mm(mixed_c, one_hot(out_order())).astype(BF)
    out_grad = mm_tn(out_turned, branch_grad).astype(BF)
    out_chunk = out_grad.reshape(8, 48, 2, HALF).transpose(0, 2, 1, 3).reshape(4, 192, HALF)
    out_rows = lax.dynamic_slice_in_dim(out_full, core * HALF, HALF, 0)
    mixed_grad = mm_nt(branch_grad, out_rows).astype(BF).reshape(by_head)
    values_grad = jnp.einsum("phqk,pqhd->pkhd", probs_low, mixed_grad, preferred_element_type=F32)
    probs_grad = jnp.einsum("pqhd,pkhd->phqk", mixed_grad, values, preferred_element_type=F32)
    centre = jnp.sum(probs * probs_grad, axis=-1, keepdims=True)
    dots_grad = (probs * (probs_grad - centre) * HEAD**-0.5).astype(BF)
    query_grad = jnp.einsum("phqk,pkhd->pqhd", dots_grad, keys, preferred_element_type=F32)
    keys_grad = jnp.einsum("phqk,pqhd->pkhd", dots_grad, query, preferred_element_type=F32)
    flat = (2 * PACK, HALF)
    query_grad = rotate(query_grad, cosine, -sine).astype(BF).reshape(flat)
    keys_grad = rotate(keys_grad, cosine, -sine).astype(BF).reshape(flat)
    values_grad = values_grad.astype(BF).reshape(flat)
    one_turned = mm(normed, turn).astype(BF)
    qkv_chunks = column_chunks(
        one_turned, jnp.concatenate([query_grad, keys_grad, values_grad], axis=1)
    )
    one_part = (
        mm_nt(query_grad, qkv_c[0]) + mm_nt(keys_grad, qkv_c[1]) + mm_nt(values_grad, qkv_c[2])
    )
    normed_grad = own_pack(one_part) + swap_core(other_pack(one_part))
    own_inputs = own_pack(inputs)
    own_scale = own_pack(scale_one)
    input_grad = own_pack(middle_grad) + norm_backward(
        own_inputs, own_scale, gains_full[0], normed_grad
    )
    gain_local = jnp.stack(
        [
            jnp.sum(normed_grad * own_inputs * own_scale, axis=0),
            jnp.sum(own_pack(normed_two_grad * middle * scale_two), axis=0),
        ]
    )
    gain_rows = (
        gain_local.reshape(2, 4, 4, 4, 2, 6).transpose(2, 3, 0, 1, 4, 5).reshape(4, 4, 1, 96)
    )
    gain_rows = jnp.pad(gain_rows, ((0, 0), (0, 0), (0, 15), (0, HALF - 96))).astype(BF)
    first_chunks = jnp.concatenate([qkv_chunks, out_chunk[None]])
    first_chunks = jnp.concatenate([first_chunks, gain_rows], axis=2)
    first_rows = units_first(first_chunks)

    down_rows = units_first(down_rows)
    gate_rows = units_first(gate_rows)
    up_rows = scatter_sum(up_rows, "x").astype(BF)
    first_rows = scatter_sum(first_rows, "x").astype(BF)
    gain_part = first_rows[192, :96].reshape(2, 4, 12).transpose(1, 0, 2).reshape(4, 1, 24)
    gain_part = jnp.pad(gain_part, ((0, 0), (0, 15), (0, HALF - 24)))
    planes = jnp.stack([first_rows[:192], gate_rows, up_rows, down_rows])
    planes = jnp.concatenate([planes, gain_part], axis=1)
    summed = scatter_sum(planes, "z")

    rows = summed[:192].reshape(2, 96, HALF)
    keep = lax.dynamic_index_in_dim(rows, core, 0, keepdims=False)
    send = lax.dynamic_index_in_dim(rows, 1 - core, 0, keepdims=False)
    gain_sums = summed[192, :24].reshape(2, 2, 6).transpose(1, 0, 2)
    gain_keep = lax.dynamic_index_in_dim(gain_sums, core, 0, keepdims=False)
    gain_send = lax.dynamic_index_in_dim(gain_sums, 1 - core, 0, keepdims=False)
    gain_grad = gain_keep + swap_core(gain_send)
    halves = by_core(core, keep, swap_core(send))
    as_columns = jnp.concatenate([halves[0], halves[1]], axis=1)
    as_down = halves.reshape(2, 2, 48, HALF).transpose(0, 2, 1, 3).reshape(96, WIDTH)
    as_out = (
        halves.reshape(2, 2, 4, 12, HALF).transpose(2, 0, 3, 1, 4).reshape(96, WIDTH)
    )
    unit_grad = jnp.where(
        z == 3, as_down, jnp.where((z == 0) & (y == 3), as_out, as_columns)
    )

    moment_next = MOMENTUM * moment_rows + unit_grad
    own_rows = moment_next.astype(BF)
    unit = gather_xc(own_rows, core)
    tall = z == 3
    gram = jnp.where(tall, mm_tn(unit, unit), mm_nt(unit, unit))
    slot = 2 * x + core
    gram_rows = lax.dynamic_slice_in_dim(gram, slot * 96, 96, 0).astype(BF)
    gram_sum = gram_rows.astype(F32)
    for step in (1, 3, 2):
        gram_sum = gram_sum + lax.ppermute(gram_rows, "y", shift("y", step)).astype(F32)
    gram_rows = jnp.where(z == 0, gram_rows, gram_sum.astype(BF))
    gram = gather_xc(gram_rows, core)
    size = jnp.sqrt(jnp.sum(jnp.diagonal(gram).astype(F32))) + 1e-07
    scale = 1.0 / (size * size)
    square = gram.astype(F32) * scale
    low = square.astype(BF)
    square2 = mm(low, low)
    poly = POLY_CUBIC * square + POLY_QUINTIC * square2
    poly_low = poly.astype(BF)
    step_one = mm(low, poly_low)
    step_two = mm(step_one.astype(BF), poly_low)
    square = POLY_LINEAR**2 * square + 2.0 * POLY_LINEAR * step_one + step_two
    low = square.astype(BF)
    poly_next = POLY_CUBIC * square + POLY_QUINTIC * mm(low, low)
    factor = POLY_LINEAR * (poly + poly_next) + mm(poly_next.astype(BF), poly_low)
    factor = factor.astype(BF)
    factor_rows = lax.dynamic_slice_in_dim(factor, slot * 96, 96, 0)
    left = jnp.where(tall, own_rows, factor_rows)
    right = jnp.where(tall, factor, unit)
    result = (mm(left, right) + POLY_LINEAR**2 * own_rows.astype(F32)) / size

    qkv_sum, out_sum, inner_sum, down_sum = to_owners(unit_grad.astype(BF))
    qkv_turn, out_turn, inner_turn, down_turn = to_owners(result.astype(BF))
    sums = [value.astype(F32) for value in (qkv_sum, out_sum, inner_sum, down_sum)]
    moments = [
        MOMENTUM * old + new
        for old, new in zip((qkv_moment, out_moment, inner_moment, down_moment), sums)
    ]
    weights_new = [
        old * (1.0 - MUON_RATE * WEIGHT_DECAY)
        - MUON_RATE * (0.2 * math.sqrt(longest)) * turned.astype(F32)
        for old, turned, longest in (
            (qkv_weight, qkv_turn, WIDTH),
            (out_weight, out_turn, WIDTH),
            (inner_weight, inner_turn, 4 * WIDTH),
            (down_weight, down_turn, 4 * WIDTH),
        )
    ]
    gain_next = GAIN_MOMENTUM * gain_moment + gain_grad
    gains_new = gains - GAIN_RATE * gain_next
    return (
        block_output,
        input_grad,
        gain_grad,
        gain_next,
        gains_new,
        *sums,
        *weights_new,
        *moments,
    )


def solution(mesh):
    grid = Mesh(mesh.devices.reshape(4, 4, 4, 2), AXES)
    rows = P(AXES, None)
    middle = P(None, AXES)
    stacked = P(None, AXES, None)
    weights = (stacked, rows, stacked, rows)
    in_specs = (rows, rows, rows, middle, middle) + weights + weights
    out_specs = (rows, rows, middle, middle, middle) + weights * 3
    return jax.shard_map(
        per_device, mesh=grid, in_specs=in_specs, out_specs=out_specs, check_vma=False
    )
```

```python
import math

import jax
import jax.numpy as jnp
import numpy as np
from jax import lax
from jax.experimental import pallas as pl
from jax.experimental.pallas import tpu as pltpu
from jax.sharding import Mesh
from jax.sharding import PartitionSpec as P

HEAD = 64
HALF = 384
WIDTH = 768
PACK = 128
EPSILON = 1e-06
ROPE_BASE = 10000.0
MOMENTUM = 0.95
GAIN_MOMENTUM = 0.9
MUON_RATE = 0.3
GAIN_RATE = 0.001
WEIGHT_DECAY = 0.1
POLY_LINEAR = 3.4445
POLY_CUBIC = -4.775
POLY_QUINTIC = 2.0315

AXES = ("z", "y", "x", "c")
SWAP = [(0, 1), (1, 0)]
BF = jnp.bfloat16
F32 = jnp.float32


def mm(left, right):
    return jnp.dot(left, right, preferred_element_type=F32)


def mm_nt(left, right):
    return lax.dot_general(left, right, (((1,), (1,)), ((), ())), preferred_element_type=F32)


def mm_tn(left, right):
    return lax.dot_general(left, right, (((0,), (0,)), ((), ())), preferred_element_type=F32)


def swap_core(value):
    return lax.ppermute(value, "c", SWAP)


def by_core(core, own, other):
    return jnp.where(core == 0, jnp.stack([own, other]), jnp.stack([other, own]))


def shift(axis, step):
    return [(i, (i + step) % 4) for i in range(4)]


def scatter_sum(chunks, axis):
    me = lax.axis_index(axis)
    total = lax.dynamic_index_in_dim(chunks, me, 0, keepdims=False).astype(F32)
    for step in (1, 3, 2):
        piece = lax.dynamic_index_in_dim(chunks, (me + step) % 4, 0, keepdims=False)
        total = total + lax.ppermute(piece, axis, shift(axis, step)).astype(F32)
    return total


def gather_four(value, axis):
    me = lax.axis_index(axis)
    full = jnp.zeros((4,) + value.shape, value.dtype)
    full = lax.dynamic_update_index_in_dim(full, value, me, 0)
    for step in (1, 3, 2):
        got = lax.ppermute(value, axis, shift(axis, step))
        full = lax.dynamic_update_index_in_dim(full, got, (me + 4 - step) % 4, 0)
    return full


def exchange(value, axis):
    me = lax.axis_index(axis)
    kept = lax.dynamic_index_in_dim(value, me, 0, keepdims=False)
    full = lax.dynamic_update_index_in_dim(jnp.zeros_like(value), kept, me, 0)
    for step in (1, 3, 2):
        piece = lax.dynamic_index_in_dim(value, (me + step) % 4, 0, keepdims=False)
        got = lax.ppermute(piece, axis, shift(axis, step))
        full = lax.dynamic_update_index_in_dim(full, got, (me + 4 - step) % 4, 0)
    return full


def one_hot(order):
    table = np.zeros((len(order), len(order)), np.float32)
    table[np.arange(len(order)), np.asarray(order)] = 1.0
    return jnp.asarray(table, BF)


def norm_order():
    grid = np.arange(WIDTH).reshape(4, 4, 4, 2, 6)
    return grid.transpose(2, 3, 1, 0, 4).reshape(-1)


def out_order():
    grid = np.arange(HALF).reshape(2, 4, 4, 2, 6)
    return grid.transpose(2, 3, 1, 0, 4).reshape(-1)


def down_order():
    grid = np.arange(HALF).reshape(2, 4, 2, 24)
    return grid.transpose(1, 2, 0, 3).reshape(-1)


def segment_table(lengths, count):
    ends = jnp.cumsum(lengths, dtype=jnp.int32)
    places = jnp.arange(count, dtype=jnp.int32)
    segment = jnp.sum((places[:, None] >= ends[None, :]).astype(jnp.int32), axis=1, dtype=jnp.int32)
    starts = ends - lengths
    slots = jnp.arange(lengths.shape[0], dtype=jnp.int32)
    first = jnp.sum(
        jnp.where(segment[:, None] == slots[None, :], starts[None, :], 0), axis=1, dtype=jnp.int32
    )
    return (segment, places - first)


def norm_scale(values):
    return lax.rsqrt(jnp.mean(values * values, axis=-1, keepdims=True) + EPSILON)


def norm_backward(values, scale, gain, grad):
    scaled = grad * gain
    return scale * scaled - values * (scale * scale * scale) * jnp.mean(
        scaled * values, axis=-1, keepdims=True
    )


def to_units(qkv, out, inner, down):
    first = jnp.concatenate([qkv, out[None]])
    wide = inner.reshape(2, 6, 4, WIDTH).transpose(0, 2, 1, 3)
    pieces = jnp.concatenate([first[None], wide, down.reshape(1, 4, 6, WIDTH)])
    got = exchange(pieces, "z")
    turned = jnp.where(lax.axis_index("z") == 3, got, got.transpose(1, 0, 2, 3))
    return exchange(turned, "y").reshape(96, WIDTH)


def to_owners(rows, planes_last):
    sent = rows.reshape(2, 4, 4, 6, WIDTH).swapaxes(0, 1)
    got = exchange(sent, "y").swapaxes(0, 1)
    turned = jnp.where(planes_last, got, got.swapaxes(1, 2))
    back = exchange(turned.swapaxes(0, 1), "z").swapaxes(0, 1)
    return back.astype(F32)


def owned_parts(rows):
    inner = rows[1:3].transpose(0, 2, 1, 3).reshape(2, 6, 4 * WIDTH)
    return rows[0, :3], rows[0, 3], inner, rows[3].reshape(24, WIDTH)


def rotation_tables():
    freq = ROPE_BASE ** (-np.arange(HEAD // 2) / (HEAD // 2))
    angle = np.arange(PACK)[:, None] * freq[None, :]
    cosine = np.tile(np.cos(angle), (1, 12))
    sine = np.tile(np.concatenate([-np.sin(angle), np.sin(angle)], axis=1), (1, 6))
    return jnp.asarray(cosine, F32), jnp.asarray(sine, F32)


def blocks_of(grid, group, part):
    block = lax.dynamic_slice(grid, (0, group, part * 48, 0), (16, 1, 48, HALF))
    return block.reshape(WIDTH, HALF)


def tall_blocks(grid, block, core):
    tall = grid.reshape(4, 2, 8, 2, 208, HALF)
    return [
        lax.dynamic_slice(
            tall, (block, core, 0, half, 144, 0), (1, 1, 8, 1, 48, HALF)
        ).reshape(HALF, HALF)
        for half in range(2)
    ]


def heads_of(values):
    return values.reshape(2, PACK, HALF // HEAD, HEAD)


def turn_rows(order_hot, values):
    return mm_nt(order_hot, values).astype(BF)


def attend(place, tokens, gain, cosine, sine, mask, grid, turn):
    core = place[0]
    inputs = tokens.astype(F32)
    normed = (inputs * norm_scale(inputs) * gain).astype(BF)
    weights = [blocks_of(grid, 2 * index + core, 0) for index in range(3)]
    query = rotate(mm(normed, weights[0]), cosine, sine).astype(BF)
    keys = rotate(mm(normed, weights[1]), cosine, sine).astype(BF)
    values = mm(normed, weights[2]).astype(BF)
    dots = jnp.einsum(
        "pqhd,pkhd->phqk", heads_of(query), heads_of(keys), preferred_element_type=F32
    )
    dots = jnp.where(mask[:, None] > 0.0, dots * HEAD**-0.5, -1e30)
    chances = jnp.exp(dots - jnp.max(dots, axis=-1, keepdims=True))
    chances = chances / jnp.sum(chances, axis=-1, keepdims=True)
    mixed = jnp.einsum(
        "phqk,pkhd->pqhd", chances.astype(BF), heads_of(values), preferred_element_type=F32
    )
    mixed = mixed.astype(BF).reshape(2 * PACK, HALF)
    return mixed, query, keys, values, chances, turn_rows(turn, normed), weights


def by_slots(values, at):
    return [lax.dynamic_index_in_dim(values, (at + step) % 4, 0, keepdims=False) for step in range(4)]


def gated(place, tokens, own_mixed, other_mixed, cot, gain, grid, turn, turn_down):
    core, x, y = place[0], place[1], place[2]
    both = by_core(core, own_mixed, other_mixed)
    mixed = jnp.concatenate([both[0], both[1]], axis=1)
    out_full = jnp.concatenate([blocks_of(grid, 6, 0), blocks_of(grid, 7, 0)], axis=1)
    middle = tokens.astype(F32) + mm(mixed, out_full)
    scale = norm_scale(middle)
    low = (middle * scale * gain).astype(BF)
    turned = turn_rows(turn, low)
    two_part, down_part = 0.0, 0.0
    gates, downs, ups = [], [], []
    for slot in range(4):
        block = (y + slot) % 4
        w_gate, w_up = blocks_of(grid, 2 * block + core, 1), blocks_of(grid, 2 * block + core, 2)
        w_down = jnp.concatenate(tall_blocks(grid, block, core), axis=1)
        gate = mm(low, w_gate)
        upward = mm(low, w_up)
        sigma = jax.nn.sigmoid(gate)
        activated = gate * sigma
        hidden = (activated * upward).astype(BF)
        hidden_grad = mm_nt(cot, w_down)
        gate_grad = (hidden_grad * upward * (sigma * (1.0 + gate * (1.0 - sigma)))).astype(BF)
        up_grad = (hidden_grad * activated).astype(BF)
        two_part = two_part + (mm_nt(gate_grad, w_gate) + mm_nt(up_grad, w_up))
        down_part = down_part + mm(hidden, w_down)
        ups.append(mm(turned, up_grad).astype(BF).reshape(4, 192, HALF))
        gates.append(mm(turned, gate_grad).astype(BF).reshape(4, 192, HALF))
        down = mm(turn_rows(turn_down, hidden), cot).astype(BF)
        down = down.reshape(8, 48, 2, HALF).transpose(0, 2, 1, 3).reshape(4, 192, HALF)
        downs.append(down)
    gain_part = jnp.sum(two_part * middle * scale, axis=0, keepdims=True)
    gates = by_slots(jnp.stack(gates, axis=1), x)
    downs = by_slots(jnp.stack(downs, axis=1), x)
    return middle, two_part, down_part, gain_part, gates, downs, ups


def attend_back(
    place, tokens, middle, own_part, other_part, cot, gains, gain_two, cosine, sine, grid,
    mixed, query, keys, values, probs, one_turned, turn_out, weights,
):
    core, y = place[0], place[2]
    grad = cot.astype(F32) + norm_backward(
        middle, norm_scale(middle), gains[1:2, :], own_part + other_part
    )
    branch_grad = grad.astype(BF)
    half = grid.reshape(2, 8, 8, 208, HALF)
    out_rows = [
        lax.dynamic_slice(half, (core, 0, group, 0, 0), (1, 8, 1, 48, HALF)).reshape(HALF, HALF)
        for group in (6, 7)
    ]
    mixed_grad = mm_nt(branch_grad, jnp.concatenate(out_rows, axis=1)).astype(BF)
    out_grad = mm(turn_rows(turn_out, mixed), branch_grad).astype(BF)
    out_grad = out_grad.reshape(8, 48, 2, HALF).transpose(0, 2, 1, 3).reshape(4, 192, HALF)
    grads = heads_of(mixed_grad)
    values_grad = jnp.einsum(
        "phqk,pqhd->pkhd", probs.astype(BF), grads, preferred_element_type=F32
    )
    probs_grad = jnp.einsum("pqhd,pkhd->phqk", grads, heads_of(values), preferred_element_type=F32)
    centre = jnp.sum(probs * probs_grad, axis=-1, keepdims=True)
    dots = (probs * (probs_grad - centre) * HEAD**-0.5).astype(BF)
    query_grad = jnp.einsum("phqk,pkhd->pqhd", dots, heads_of(keys), preferred_element_type=F32)
    keys_grad = jnp.einsum("phqk,pqhd->pkhd", dots, heads_of(query), preferred_element_type=F32)
    flat = (2 * PACK, HALF)
    low = [
        rotate(query_grad.reshape(flat), cosine, -sine).astype(BF),
        rotate(keys_grad.reshape(flat), cosine, -sine).astype(BF),
        values_grad.reshape(flat).astype(BF),
    ]
    total = sum(mm_nt(part, weight) for part, weight in zip(low, weights))
    inputs = tokens.astype(F32)
    gain_one = jnp.sum(total * inputs * norm_scale(inputs), axis=0, keepdims=True)
    tail = jnp.concatenate([gain_one, gain_two]).reshape(4, HALF)
    tail = jnp.pad(tail, ((0, 12), (0, 0))).astype(BF)
    chunks = [mm(one_turned, part).astype(BF).reshape(4, 192, HALF) for part in low] + [out_grad]
    tails = jnp.broadcast_to(tail, (4, 16, HALF))
    slots = by_slots(jnp.stack(chunks), y)
    slots = [jnp.concatenate([slot, tails], axis=1) for slot in slots]
    return grad, total, slots


def rotate(values, cosine, sine):
    parts = values.reshape(values.shape[0], -1, 2, HEAD // 2)
    partner = jnp.flip(parts, axis=2).reshape(values.shape)
    return values * cosine + partner * sine


def flat(ref):
    block = ref[...]
    return block.reshape(block.shape[0] * block.shape[1], block.shape[2])


def limits(**more):
    return pltpu.CompilerParams(vmem_limit_bytes=56 * 2**20, **more)


def bf_array(*shape):
    return jax.ShapeDtypeStruct(shape, BF)


def f32_array(*shape):
    return jax.ShapeDtypeStruct(shape, F32)


def whole_of(*shape):
    return pl.BlockSpec(shape, lambda step, place: (0,) * len(shape))


def gram_kernel(place, own_line, other_line, unit, gram_rows, full):
    core = place[0]
    slot = 2 * place[1] + core
    for index in range(4):
        unit[2 * index + core] = own_line[index]
        unit[2 * index + 1 - core] = other_line[index]

    @pl.when(place[3] != 3)
    def _():
        gram_rows[...] = mm_nt(unit[slot], flat(unit)).astype(BF)

    @pl.when(place[3] == 3)
    def _():
        rows = flat(unit)
        full[...] = mm_tn(rows, rows).reshape(8, 96, WIDTH)
        gram_rows[...] = full[slot].astype(BF)


def polish_kernel(place, own_line, other_line, unit, result, gram, low, poly, square):
    core = place[0]
    slot = 2 * place[1] + core
    for index in range(4):
        gram[2 * index + core] = own_line[index]
        gram[2 * index + 1 - core] = other_line[index]
    trace = jnp.zeros((1, 1), F32)
    for index in range(8):
        rows = lax.broadcasted_iota(jnp.int32, (96, WIDTH), 0) + index * 96
        cols = lax.broadcasted_iota(jnp.int32, (96, WIDTH), 1)
        part = jnp.where(rows == cols, gram[index].astype(F32), 0.0)
        part = jnp.sum(part, axis=1, keepdims=True)
        trace = trace + jnp.sum(part, axis=0, keepdims=True)
    size = jnp.sqrt(trace) + 1e-07
    scale = 1.0 / (size * size)

    def each(body):
        lax.fori_loop(0, 4, lambda index, carry: (body(index), carry)[1], 0)

    def two(ref, index):
        return ref[pl.ds(2 * index, 2)].reshape(192, WIDTH)

    def put(ref, index, value):
        ref[pl.ds(2 * index, 2)] = value.astype(ref.dtype).reshape(2, 96, WIDTH)

    def first(index):
        rows = two(gram, index)
        value = POLY_CUBIC * (rows.astype(F32) * scale) + POLY_QUINTIC * (
            mm(rows, flat(gram)) * (scale * scale)
        )
        put(poly, index, value)

    each(first)

    def second(index):
        rows = two(gram, index)
        one = mm(rows, flat(poly)) * scale
        value = (
            POLY_LINEAR**2 * (rows.astype(F32) * scale)
            + 2.0 * POLY_LINEAR * one
            + mm(one.astype(BF), flat(poly))
        )
        put(square, index, value)
        put(low, index, value)

    each(second)

    def third(index):
        value = POLY_CUBIC * two(square, index) + POLY_QUINTIC * mm(two(low, index), flat(low))
        total = POLY_LINEAR * (two(poly, index).astype(F32) + value) + mm(
            value.astype(BF), flat(poly)
        )
        put(gram, index, total)

    each(third)
    own = unit[slot]
    base = POLY_LINEAR**2 * own.astype(F32)

    @pl.when(place[3] != 3)
    def _():
        result[...] = ((mm(gram[slot], flat(unit)) + base) / size).astype(BF)

    @pl.when(place[3] == 3)
    def _():
        result[...] = ((mm(own, flat(gram)) + base) / size).astype(BF)


def gram_of(place, own_line, other_line):
    return pl.pallas_call(
        gram_kernel,
        out_shape=(bf_array(8, 96, WIDTH), bf_array(96, WIDTH)),
        grid_spec=pltpu.PrefetchScalarGridSpec(
            num_scalar_prefetch=1,
            grid=(1,),
            in_specs=[whole_of(4, 96, WIDTH)] * 2,
            out_specs=[whole_of(8, 96, WIDTH), whole_of(96, WIDTH)],
            scratch_shapes=[pltpu.VMEM((8, 96, WIDTH), F32)],
        ),
        compiler_params=limits(),
        cost_estimate=pl.CostEstimate(flops=10**9, bytes_accessed=3 * 10**6, transcendentals=0),
        name="gram",
    )(place, own_line, other_line)


def polish(place, own_line, other_line, unit):
    return pl.pallas_call(
        polish_kernel,
        out_shape=bf_array(96, WIDTH),
        grid_spec=pltpu.PrefetchScalarGridSpec(
            num_scalar_prefetch=1,
            grid=(1,),
            in_specs=[whole_of(4, 96, WIDTH)] * 2 + [whole_of(8, 96, WIDTH)],
            out_specs=whole_of(96, WIDTH),
            scratch_shapes=[
                pltpu.VMEM((8, 96, WIDTH), BF),
                pltpu.VMEM((8, 96, WIDTH), BF),
                pltpu.VMEM((8, 96, WIDTH), BF),
                pltpu.VMEM((8, 96, WIDTH), F32),
            ],
        ),
        compiler_params=limits(),
        cost_estimate=pl.CostEstimate(
            flops=5 * 10**9, bytes_accessed=4 * 10**6, transcendentals=0
        ),
        name="polish",
    )(place, own_line, other_line, unit)


def sum_slots(slots, axis):
    total = slots[0].astype(F32)
    for step in (1, 3, 2):
        total = total + lax.ppermute(slots[step], axis, shift(axis, step)).astype(F32)
    return total


def per_device(
    tokens,
    cotangent,
    lengths,
    gains,
    gain_moment,
    qkv_weight,
    out_weight,
    inner_weight,
    down_weight,
    qkv_moment,
    out_moment,
    inner_moment,
    down_moment,
):
    z, y, x, core = (lax.axis_index(name) for name in AXES)
    place = jnp.stack([core, x, y, z]).astype(jnp.int32)
    first = jnp.concatenate([qkv_weight, out_weight[None]]).astype(BF)
    first = first.reshape(4, 6, 2, HALF).transpose(0, 2, 1, 3)
    wide = inner_weight.astype(BF).reshape(2, 6, 4, 2, HALF).transpose(0, 2, 3, 1, 4)
    blocks = jnp.stack([first, wide[0], wide[1]], axis=2).reshape(8, 3, 6, HALF)
    blocks = lax.all_to_all(blocks, ("x", "c"), split_axis=0, concat_axis=0, tiled=True)
    blocks = blocks.transpose(1, 0, 2, 3).reshape(144, HALF)
    down_low = down_weight.astype(BF)
    down_keep = jnp.where(core == 0, down_low[:, :HALF], down_low[:, HALF:])
    down_send = jnp.where(core == 0, down_low[:, HALF:], down_low[:, :HALF])
    down_piece = by_core(core, down_keep, swap_core(down_send)).reshape(48, HALF)
    gain_piece = lax.dynamic_update_slice_in_dim(
        jnp.zeros((2, WIDTH), F32), gains, lax.axis_index(AXES) * 6, 1
    )
    gain_piece = jnp.pad(gain_piece.reshape(4, HALF), ((0, 12), (0, 0))).astype(BF)
    piece = jnp.concatenate([blocks, down_piece, gain_piece])
    whole = lax.all_gather(piece, AXES, axis=0, tiled=True)
    tokens2 = by_core(core, tokens, swap_core(tokens)).reshape(2 * PACK, WIDTH)
    cot2 = by_core(core, cotangent, swap_core(cotangent)).reshape(2 * PACK, WIDTH)
    lengths2 = by_core(core, lengths[0], swap_core(lengths[0].astype(F32)).astype(jnp.int32))
    moment_rows = to_units(qkv_moment, out_moment, inner_moment, down_moment)
    segment, position = jax.vmap(lambda row: segment_table(row, PACK))(lengths2)
    tables = rotation_tables()
    cosine, sine = (table[position.reshape(2 * PACK)] for table in tables)
    places = jnp.arange(PACK, dtype=jnp.int32)
    allowed = (segment[:, :, None] == segment[:, None, :]) & (places[None, :] <= places[:, None])
    mask = allowed.astype(F32)
    turn, turn_out, turn_down = (
        one_hot(order()) for order in (norm_order, out_order, down_order)
    )
    whole, moment_rows, tokens2, cot2, cosine, sine, mask = lax.optimization_barrier(
        (whole, moment_rows, tokens2, cot2, cosine, sine, mask)
    )

    grid = whole.reshape(16, 8, 208, HALF)
    gains_full = jnp.sum(grid[:, :, 192:196].astype(F32), axis=(0, 1)).reshape(2, WIDTH)
    mixed, query, keys, values, probs, one_turned, weights = attend(
        place, tokens2, gains_full[0:1], cosine, sine, mask, grid, turn
    )
    results = gated(
        place, tokens2, mixed, swap_core(mixed), cot2, gains_full[1:2], grid, turn, turn_down
    )
    middle, two_part, down_part, gain_two, gate_slots, down_slots, up_slots = results
    two_other = swap_core(two_part)

    def own_pack(value):
        return lax.dynamic_slice_in_dim(value, core * PACK, PACK, 0)

    def other_pack(value):
        return lax.dynamic_slice_in_dim(value, (1 - core) * PACK, PACK, 0)

    down_rows = sum_slots(down_slots, "x").astype(BF)
    up_rows = sum_slots(up_slots, "y").astype(BF)
    gate_rows = sum_slots(gate_slots, "x").astype(BF)
    results = attend_back(
        place, tokens2, middle, two_part, two_other, cot2, gains_full, gain_two, cosine, sine,
        grid, mixed, query, keys, values, probs, one_turned, turn_out, weights,
    )
    middle_grad, one_part, first_slots = results
    first_rows = sum_slots(first_slots, "y").astype(BF)

    block_output = (
        own_pack(middle) + own_pack(down_part) + swap_core(other_pack(down_part))
    ).astype(BF)
    normed_grad = own_pack(one_part) + swap_core(other_pack(one_part))
    own_inputs = tokens.astype(F32)
    input_grad = own_pack(middle_grad) + norm_backward(
        own_inputs, norm_scale(own_inputs), gains_full[0], normed_grad
    )

    down_rows = sum_slots(list(down_rows), "y").astype(BF)
    gate_rows = sum_slots(list(gate_rows), "y").astype(BF)
    up_rows = scatter_sum(up_rows, "x").astype(BF)
    first_rows = scatter_sum(first_rows, "x").astype(BF)
    tail = first_rows[192:]
    planes = jnp.stack(
        [first_rows]
        + [jnp.concatenate([part, tail]) for part in (gate_rows, up_rows, down_rows)]
    )
    summed = scatter_sum(planes, "z")

    rows = summed[:192].reshape(2, 96, HALF)
    keep = lax.dynamic_index_in_dim(rows, core, 0, keepdims=False)
    send = lax.dynamic_index_in_dim(rows, 1 - core, 0, keepdims=False)
    got = swap_core(jnp.concatenate([send, summed[192:200]]))
    gain_sums = (summed[192:196] + got[96:100]).reshape(2, WIDTH)
    gain_grad = lax.dynamic_slice_in_dim(gain_sums, lax.axis_index(AXES) * 6, 6, 1)
    halves = by_core(core, keep, got[:96])
    as_columns = jnp.concatenate([halves[0], halves[1]], axis=1)
    as_down = halves.reshape(2, 2, 48, HALF).transpose(0, 2, 1, 3).reshape(96, WIDTH)
    as_out = halves.reshape(2, 2, 4, 12, HALF).transpose(2, 0, 3, 1, 4).reshape(96, WIDTH)
    unit_grad = jnp.where(z == 3, as_down, jnp.where((z == 0) & (y == 3), as_out, as_columns))

    moment_next = MOMENTUM * moment_rows + unit_grad
    line = gather_four(moment_next.astype(BF), "x")
    unit, gram_rows = gram_of(place, line, swap_core(line))
    gram_sum = gram_rows.astype(F32)
    for step in (1, 3, 2):
        pairs = [
            (4 * plane + at, 4 * plane + (at + step) % 4) for plane in (1, 2, 3) for at in range(4)
        ]
        gram_sum = gram_sum + lax.ppermute(gram_rows, ("z", "y"), pairs).astype(F32)
    gram_rows = gram_sum.astype(BF)
    line = gather_four(gram_rows, "x")
    result = polish(place, line, swap_core(line), unit)

    returned = to_owners(jnp.stack([unit_grad.astype(BF), result]), z == 3)
    sums, turned_parts = lax.optimization_barrier(
        (owned_parts(returned[0]), owned_parts(returned[1]))
    )
    moments = [
        MOMENTUM * old + new
        for old, new in zip((qkv_moment, out_moment, inner_moment, down_moment), sums)
    ]
    weights_new = [
        old * (1.0 - MUON_RATE * WEIGHT_DECAY)
        - MUON_RATE * (0.2 * math.sqrt(longest)) * turned
        for old, turned, longest in zip(
            (qkv_weight, out_weight, inner_weight, down_weight),
            turned_parts,
            (WIDTH, WIDTH, 4 * WIDTH, 4 * WIDTH),
        )
    ]
    gain_next = GAIN_MOMENTUM * gain_moment + gain_grad
    gains_new = gains - GAIN_RATE * gain_next
    return (
        block_output,
        input_grad,
        gain_grad,
        gain_next,
        gains_new,
        *sums,
        *weights_new,
        *moments,
    )


def solution(mesh):
    grid = Mesh(mesh.devices.reshape(4, 4, 4, 2), AXES)
    rows = P(AXES, None)
    middle = P(None, AXES)
    stacked = P(None, AXES, None)
    weights = (stacked, rows, stacked, rows)
    in_specs = (rows, rows, rows, middle, middle) + weights + weights
    out_specs = (rows, rows, middle, middle, middle) + weights * 3
    return jax.shard_map(
        per_device, mesh=grid, in_specs=in_specs, out_specs=out_specs, check_vma=False
    )
```

```python
import math

import jax
import jax.numpy as jnp
import numpy as np
from jax import lax
from jax.experimental import pallas as pl
from jax.sharding import Mesh
from jax.sharding import PartitionSpec as P

HEAD = 64
HALF = 384
WIDTH = 768
PACK = 128
EPSILON = 1e-06
ROPE_BASE = 10000.0
MOMENTUM = 0.95
GAIN_MOMENTUM = 0.9
MUON_RATE = 0.3
GAIN_RATE = 0.001
WEIGHT_DECAY = 0.1
POLY_LINEAR = 3.4445
POLY_CUBIC = -4.775
POLY_QUINTIC = 2.0315

AXES = ("z", "y", "x", "c")
SWAP = [(0, 1), (1, 0)]
BF = jnp.bfloat16
F32 = jnp.float32


def mm(left, right):
    return jnp.dot(left, right, preferred_element_type=F32)


def mm_nt(left, right):
    return lax.dot_general(left, right, (((1,), (1,)), ((), ())), preferred_element_type=F32)


def mm_tn(left, right):
    return lax.dot_general(left, right, (((0,), (0,)), ((), ())), preferred_element_type=F32)


def swap_core(value):
    return lax.ppermute(value, "c", SWAP)


def by_core(core, own, other):
    return jnp.where(core == 0, jnp.stack([own, other]), jnp.stack([other, own]))


def shift(axis, step):
    return [(i, (i + step) % 4) for i in range(4)]


def scatter_sum(chunks, axis):
    me = lax.axis_index(axis)
    total = lax.dynamic_index_in_dim(chunks, me, 0, keepdims=False).astype(F32)
    for step in (1, 3, 2):
        piece = lax.dynamic_index_in_dim(chunks, (me + step) % 4, 0, keepdims=False)
        total = total + lax.ppermute(piece, axis, shift(axis, step)).astype(F32)
    return total


def gather_four(value, axis):
    me = lax.axis_index(axis)
    full = jnp.zeros((4,) + value.shape, value.dtype)
    full = lax.dynamic_update_index_in_dim(full, value, me, 0)
    for step in (1, 3, 2):
        got = lax.ppermute(value, axis, shift(axis, step))
        full = lax.dynamic_update_index_in_dim(full, got, (me + 4 - step) % 4, 0)
    return full


def exchange(value, axis):
    me = lax.axis_index(axis)
    kept = lax.dynamic_index_in_dim(value, me, 0, keepdims=False)
    full = lax.dynamic_update_index_in_dim(jnp.zeros_like(value), kept, me, 0)
    for step in (1, 3, 2):
        piece = lax.dynamic_index_in_dim(value, (me + step) % 4, 0, keepdims=False)
        got = lax.ppermute(piece, axis, shift(axis, step))
        full = lax.dynamic_update_index_in_dim(full, got, (me + 4 - step) % 4, 0)
    return full


def one_hot(order):
    table = np.zeros((len(order), len(order)), np.float32)
    table[np.arange(len(order)), np.asarray(order)] = 1.0
    return jnp.asarray(table, BF)


def norm_order():
    grid = np.arange(WIDTH).reshape(4, 4, 4, 2, 6)
    return grid.transpose(2, 3, 1, 0, 4).reshape(-1)


def out_order():
    grid = np.arange(HALF).reshape(2, 4, 4, 2, 6)
    return grid.transpose(2, 3, 1, 0, 4).reshape(-1)


def down_order():
    grid = np.arange(HALF).reshape(2, 4, 2, 24)
    return grid.transpose(1, 2, 0, 3).reshape(-1)


def segment_table(lengths, count):
    ends = jnp.cumsum(lengths, dtype=jnp.int32)
    places = jnp.arange(count, dtype=jnp.int32)
    segment = jnp.sum((places[:, None] >= ends[None, :]).astype(jnp.int32), axis=1, dtype=jnp.int32)
    starts = ends - lengths
    slots = jnp.arange(lengths.shape[0], dtype=jnp.int32)
    first = jnp.sum(
        jnp.where(segment[:, None] == slots[None, :], starts[None, :], 0), axis=1, dtype=jnp.int32
    )
    return (segment, places - first)


def norm_scale(values):
    return lax.rsqrt(jnp.mean(values * values, axis=-1, keepdims=True) + EPSILON)


def norm_backward(values, scale, gain, grad):
    scaled = grad * gain
    return scale * scaled - values * (scale * scale * scale) * jnp.mean(
        scaled * values, axis=-1, keepdims=True
    )


def to_units(qkv, out, inner, down):
    first = jnp.concatenate([qkv, out[None]])
    wide = inner.reshape(2, 6, 4, WIDTH).transpose(0, 2, 1, 3)
    pieces = jnp.concatenate([first[None], wide, down.reshape(1, 4, 6, WIDTH)])
    got = exchange(pieces, "z")
    turned = jnp.where(lax.axis_index("z") == 3, got, got.transpose(1, 0, 2, 3))
    return exchange(turned, "y").reshape(96, WIDTH)


def to_owners(rows, planes_last):
    sent = rows.reshape(2, 4, 4, 6, WIDTH).swapaxes(0, 1)
    got = exchange(sent, "y").swapaxes(0, 1)
    turned = jnp.where(planes_last, got, got.swapaxes(1, 2))
    back = exchange(turned.swapaxes(0, 1), "z").swapaxes(0, 1)
    return back.astype(F32)


def owned_parts(rows):
    inner = rows[1:3].transpose(0, 2, 1, 3).reshape(2, 6, 4 * WIDTH)
    return rows[0, :3], rows[0, 3], inner, rows[3].reshape(24, WIDTH)


def rotation_tables():
    freq = ROPE_BASE ** (-np.arange(HEAD // 2) / (HEAD // 2))
    angle = np.arange(PACK)[:, None] * freq[None, :]
    return jnp.asarray(np.cos(angle), F32), jnp.asarray(np.sin(angle), F32)


def blocks_of(grid, group, part):
    block = lax.dynamic_slice(grid, (0, group, part * 48, 0), (16, 1, 48, HALF))
    return block.reshape(WIDTH, HALF)


def tall_blocks(grid, block, core):
    tall = grid.reshape(4, 2, 8, 2, 208, HALF)
    return [
        lax.dynamic_slice(
            tall, (block, core, 0, half, 144, 0), (1, 1, 8, 1, 48, HALF)
        ).reshape(HALF, HALF)
        for half in range(2)
    ]


def heads_of(values):
    return values.reshape(2, PACK, HALF // HEAD, HEAD)


def turn_rows(order_hot, values):
    return mm_nt(order_hot, values).astype(BF)


def attend(place, tokens, gain, cosine, sine, mask, grid, turn):
    core = place[0]
    inputs = tokens.astype(F32)
    normed = (inputs * norm_scale(inputs) * gain).astype(BF)
    weights = [blocks_of(grid, 2 * index + core, 0) for index in range(3)]
    query = rotate(heads_of(mm(normed, weights[0])), cosine, sine).astype(BF)
    keys = rotate(heads_of(mm(normed, weights[1])), cosine, sine).astype(BF)
    values = heads_of(mm(normed, weights[2]).astype(BF))
    dots = jnp.einsum("pqhd,pkhd->phqk", query, keys, preferred_element_type=F32)
    dots = jnp.where(mask[:, None] > 0.0, dots * HEAD**-0.5, -1e30)
    chances = jnp.exp(dots - jnp.max(dots, axis=-1, keepdims=True))
    chances = chances / jnp.sum(chances, axis=-1, keepdims=True)
    mixed = jnp.einsum(
        "phqk,pkhd->pqhd", chances.astype(BF), values, preferred_element_type=F32
    )
    mixed = mixed.astype(BF).reshape(2 * PACK, HALF)
    return mixed, query, keys, values, chances, turn_rows(turn, normed), weights


def by_slots(values, at):
    return [lax.dynamic_index_in_dim(values, (at + step) % 4, 0, keepdims=False) for step in range(4)]


def gated(place, tokens, own_mixed, other_mixed, cot, gain, grid, turn, turn_down):
    core, x, y = place[0], place[1], place[2]
    both = by_core(core, own_mixed, other_mixed)
    mixed = jnp.concatenate([both[0], both[1]], axis=1)
    out_full = jnp.concatenate([blocks_of(grid, 6, 0), blocks_of(grid, 7, 0)], axis=1)
    middle = tokens.astype(F32) + mm(mixed, out_full)
    scale = norm_scale(middle)
    low = (middle * scale * gain).astype(BF)
    weights, parts, hiddens = [], [], []
    for slot in range(4):
        group = 2 * ((y + slot) % 4) + core
        w_gate, w_up = blocks_of(grid, group, 1), blocks_of(grid, group, 2)
        gate = mm(low, w_gate)
        upward = mm(low, w_up)
        sigma = jax.nn.sigmoid(gate)
        activated = gate * sigma
        weights.append((w_gate, w_up))
        parts.append((gate, upward, sigma, activated))
        hiddens.append((activated * upward).astype(BF))
    turned = jnp.stack([turn_rows(turn_down, hidden) for hidden in hiddens])
    turned = turned.reshape(4, 4, 96, 2 * PACK)
    downs = [
        mm(
            lax.dynamic_index_in_dim(turned, (x + slot) % 4, 1, keepdims=False).reshape(HALF, -1),
            cot,
        ).astype(BF)
        for slot in range(4)
    ]
    cot, downs = lax.optimization_barrier((cot, downs))
    two_part, down_part = 0.0, 0.0
    gate_grads, up_grads = [], []
    for slot in range(4):
        gate, upward, sigma, activated = parts[slot]
        w_gate, w_up = weights[slot]
        w_down = jnp.concatenate(tall_blocks(grid, (y + slot) % 4, core), axis=1)
        hidden_grad = mm_nt(cot, w_down)
        gate_grad = (hidden_grad * upward * (sigma * (1.0 + gate * (1.0 - sigma)))).astype(BF)
        up_grad = (hidden_grad * activated).astype(BF)
        two_part = two_part + (mm_nt(gate_grad, w_gate) + mm_nt(up_grad, w_up))
        down_part = down_part + mm(hiddens[slot], w_down)
        gate_grads.append(gate_grad)
        up_grads.append(up_grad)
    two_part, gate_grads, up_grads = lax.optimization_barrier((two_part, gate_grads, up_grads))
    turned = turn_rows(turn, low)
    wides = [
        mm(turned, jnp.concatenate(pair, axis=1)).astype(BF) for pair in zip(up_grads, gate_grads)
    ]
    gain_part = jnp.sum(two_part * middle * scale, axis=0, keepdims=True)
    return middle, two_part, down_part, gain_part, downs, wides


def attend_back(
    place, tokens, middle, normed_two_grad, cot, gains, gain_two, cosine, sine, grid,
    mixed, query, keys, values, probs, one_turned, turn_out, weights,
):
    core, x = place[0], place[1]
    grad = cot.astype(F32) + norm_backward(
        middle, norm_scale(middle), gains[1:2, :], normed_two_grad
    )
    branch_grad = grad.astype(BF)
    half = grid.reshape(2, 8, 8, 208, HALF)
    out_rows = [
        lax.dynamic_slice(half, (core, 0, group, 0, 0), (1, 8, 1, 48, HALF)).reshape(HALF, HALF)
        for group in (6, 7)
    ]
    mixed_grad = mm_nt(branch_grad, jnp.concatenate(out_rows, axis=1)).astype(BF)
    out_turned = turn_rows(turn_out, mixed)
    grads = heads_of(mixed_grad)
    values_grad = jnp.einsum(
        "phqk,pqhd->pkhd", probs.astype(BF), grads, preferred_element_type=F32
    )
    probs_grad = jnp.einsum("pqhd,pkhd->phqk", grads, values, preferred_element_type=F32)
    centre = jnp.sum(probs * probs_grad, axis=-1, keepdims=True)
    dots = (probs * (probs_grad - centre) * HEAD**-0.5).astype(BF)
    query_grad = jnp.einsum("phqk,pkhd->pqhd", dots, keys, preferred_element_type=F32)
    keys_grad = jnp.einsum("phqk,pqhd->pkhd", dots, query, preferred_element_type=F32)
    flat = (2 * PACK, HALF)
    low = [
        rotate(query_grad, cosine, -sine).astype(BF).reshape(flat),
        rotate(keys_grad, cosine, -sine).astype(BF).reshape(flat),
        values_grad.reshape(flat).astype(BF),
    ]
    total = sum(mm_nt(part, weight) for part, weight in zip(low, weights))
    inputs = tokens.astype(F32)
    gain_one = jnp.sum(total * inputs * norm_scale(inputs), axis=0, keepdims=True)
    tail = jnp.concatenate([gain_one, gain_two]).reshape(4, HALF)
    tail = jnp.pad(tail, ((0, 12), (0, 0))).astype(BF)
    tails = jnp.tile(tail, (1, 4))
    wide = jnp.concatenate(low, axis=1)
    slots = []
    for slot in range(4):
        at = (x + slot) % 4
        columns = mm(lax.dynamic_slice_in_dim(one_turned, at * 192, 192, 0), wide)
        rows = mm(lax.dynamic_slice_in_dim(out_turned, at * 96, 96, 0), branch_grad)
        rows = jnp.concatenate(
            [rows[48 * part : 48 * part + 48, half : half + HALF] for part in (0, 1) for half in (0, HALF)]
        )
        piece = jnp.concatenate([columns.astype(BF), rows.astype(BF)], axis=1)
        slots.append(jnp.concatenate([piece, tails]))
    return grad, total, slots


def rotate(values, cosine, sine):
    half = HEAD // 2
    first, second = values[..., :half], values[..., half:]
    return jnp.concatenate(
        [first * cosine - second * sine, second * cosine + first * sine], axis=-1
    )


def gram_of(place, own_line, other_line):
    core, x, plane = place[0], place[1], place[3]
    unit = jnp.moveaxis(by_core(core, own_line, other_line), 0, 1).reshape(WIDTH, WIDTH)
    full = jnp.where(plane == 3, mm_tn(unit, unit), mm_nt(unit, unit))
    return unit, lax.dynamic_slice_in_dim(full, (2 * x + core) * 96, 96, 0).astype(BF)


def polish(place, own_line, other_line, unit):
    core, x, plane = place[0], place[1], place[3]
    slot = 2 * x + core
    gram = jnp.moveaxis(by_core(core, own_line, other_line), 0, 1).reshape(WIDTH, WIDTH)
    at = lax.broadcasted_iota(jnp.int32, gram.shape, 0)
    diagonal = at == lax.broadcasted_iota(jnp.int32, gram.shape, 1)
    size = jnp.sqrt(jnp.sum(jnp.where(diagonal, gram.astype(F32), 0.0))) + 1e-07
    scale = 1.0 / (size * size)
    square = gram.astype(F32) * scale
    poly = POLY_CUBIC * square + POLY_QUINTIC * (mm(gram, gram) * (scale * scale))
    poly_low = poly.astype(BF)
    one = mm(gram, poly_low) * scale
    square = POLY_LINEAR**2 * square + 2.0 * POLY_LINEAR * one + mm(one.astype(BF), poly_low)
    low = square.astype(BF)
    poly_next = POLY_CUBIC * square + POLY_QUINTIC * mm(low, low)
    factor = POLY_LINEAR * (poly + poly_next) + mm(poly_next.astype(BF), poly_low)
    factor = factor.astype(BF)
    own = lax.dynamic_slice_in_dim(unit, slot * 96, 96, 0)
    left = jnp.where(plane == 3, own, lax.dynamic_slice_in_dim(factor, slot * 96, 96, 0))
    right = jnp.where(plane == 3, factor, unit)
    result = (mm(left, right) + POLY_LINEAR**2 * own.astype(F32)) / size
    return result.astype(BF)


def join_kernel(own, other, total):
    total[...] = own[...] + other[...]


def join_cores(own, other):
    return pl.pallas_call(
        join_kernel,
        out_shape=jax.ShapeDtypeStruct(own.shape, F32),
        cost_estimate=pl.CostEstimate(
            flops=5 * 10**10, bytes_accessed=3 * 10**6, transcendentals=0
        ),
        name="join_cores",
    )(own, other)


def send_slots(slots, axis):
    got = [lax.ppermute(slots[step], axis, shift(axis, step)) for step in (1, 3, 2)]
    return [slots[0]] + got


def sum_pieces(pieces):
    total = pieces[0].astype(F32)
    for piece in pieces[1:]:
        total = total + piece.astype(F32)
    return total


def sum_slots(slots, axis):
    return sum_pieces(send_slots(slots, axis))


def per_device(
    tokens,
    cotangent,
    lengths,
    gains,
    gain_moment,
    qkv_weight,
    out_weight,
    inner_weight,
    down_weight,
    qkv_moment,
    out_moment,
    inner_moment,
    down_moment,
):
    z, y, x, core = (lax.axis_index(name) for name in AXES)
    place = jnp.stack([core, x, y, z]).astype(jnp.int32)
    first = jnp.concatenate([qkv_weight, out_weight[None]]).astype(BF)
    first = first.reshape(4, 6, 2, HALF).transpose(0, 2, 1, 3)
    wide = inner_weight.astype(BF).reshape(2, 6, 4, 2, HALF).transpose(0, 2, 3, 1, 4)
    blocks = jnp.stack([first, wide[0], wide[1]], axis=2).reshape(8, 3, 6, HALF)
    blocks = lax.all_to_all(blocks, ("x", "c"), split_axis=0, concat_axis=0, tiled=True)
    blocks = blocks.transpose(1, 0, 2, 3).reshape(144, HALF)
    down_low = down_weight.astype(BF)
    down_keep = jnp.where(core == 0, down_low[:, :HALF], down_low[:, HALF:])
    down_send = jnp.where(core == 0, down_low[:, HALF:], down_low[:, :HALF])
    down_piece = by_core(core, down_keep, swap_core(down_send)).reshape(48, HALF)
    gain_piece = lax.dynamic_update_slice_in_dim(
        jnp.zeros((2, WIDTH), F32), gains, lax.axis_index(AXES) * 6, 1
    )
    gain_piece = jnp.pad(gain_piece.reshape(4, HALF), ((0, 12), (0, 0))).astype(BF)
    piece = jnp.concatenate([blocks, down_piece, gain_piece])
    whole = lax.all_gather(piece, AXES, axis=0, tiled=True)
    tokens2 = by_core(core, tokens, swap_core(tokens)).reshape(2 * PACK, WIDTH)
    cot2 = by_core(core, cotangent, swap_core(cotangent)).reshape(2 * PACK, WIDTH)
    lengths2 = by_core(core, lengths[0], swap_core(lengths[0].astype(F32)).astype(jnp.int32))
    moment_rows = to_units(qkv_moment, out_moment, inner_moment, down_moment)
    segment, position = jax.vmap(lambda row: segment_table(row, PACK))(lengths2)
    tables = rotation_tables()
    cosine, sine = (table[position][:, :, None, :] for table in tables)
    places = jnp.arange(PACK, dtype=jnp.int32)
    allowed = (segment[:, :, None] == segment[:, None, :]) & (places[None, :] <= places[:, None])
    mask = allowed.astype(F32)
    turn, turn_out, turn_down = (
        one_hot(order()) for order in (norm_order, out_order, down_order)
    )
    whole, moment_rows, tokens2, cot2, cosine, sine, mask = lax.optimization_barrier(
        (whole, moment_rows, tokens2, cot2, cosine, sine, mask)
    )

    grid = whole.reshape(16, 8, 208, HALF)
    gains_full = jnp.sum(grid[:, :, 192:196].astype(F32), axis=(0, 1)).reshape(2, WIDTH)
    mixed, query, keys, values, probs, one_turned, weights = attend(
        place, tokens2, gains_full[0:1], cosine, sine, mask, grid, turn
    )
    results = gated(
        place, tokens2, mixed, swap_core(mixed), cot2, gains_full[1:2], grid, turn, turn_down
    )
    middle, two_part, down_part, gain_two, down_slots, wide_slots = results
    two_other = swap_core(two_part)
    down_pieces = send_slots(down_slots, "x")
    wide_pieces = send_slots(wide_slots, "y")
    normed_two_grad = join_cores(two_part, two_other)

    def own_pack(value):
        return lax.dynamic_slice_in_dim(value, core * PACK, PACK, 0)

    def other_pack(value):
        return lax.dynamic_slice_in_dim(value, (1 - core) * PACK, PACK, 0)

    results = attend_back(
        place, tokens2, middle, normed_two_grad, cot2, gains_full, gain_two, cosine, sine,
        grid, mixed, query, keys, values, probs, one_turned, turn_out, weights,
    )
    middle_grad, one_part, first_slots = results
    first_slots, down_pieces, wide_pieces = lax.optimization_barrier(
        (first_slots, down_pieces, wide_pieces)
    )
    first_pieces = send_slots(first_slots, "x")
    down_rows = sum_pieces(down_pieces).astype(BF)
    wide_rows = sum_pieces(wide_pieces).astype(BF)
    first_rows = sum_pieces(first_pieces).astype(BF)

    block_output = (
        own_pack(middle) + own_pack(down_part) + swap_core(other_pack(down_part))
    ).astype(BF)
    normed_grad = own_pack(one_part) + swap_core(other_pack(one_part))
    own_inputs = tokens.astype(F32)
    input_grad = own_pack(middle_grad) + norm_backward(
        own_inputs, norm_scale(own_inputs), gains_full[0], normed_grad
    )

    wide_rows = scatter_sum(wide_rows.reshape(4, 192, WIDTH), "x").astype(BF)
    line_slots = []
    for at in range(4):
        first = lax.dynamic_slice_in_dim(first_rows, (y + at) % 4 * HALF, HALF, 1)
        down = down_rows[96 * at : 96 * at + 96]
        line_slots.append(jnp.concatenate([first, down[:, :HALF], down[:, HALF:]]))
    line_rows = sum_slots(line_slots, "y").astype(BF)
    first_rows, down_rows = line_rows[:208], line_rows[208:].reshape(2, 2, 48, HALF)
    down_rows = down_rows.transpose(1, 0, 2, 3).reshape(192, HALF)
    up_rows, gate_rows = wide_rows[:, :HALF], wide_rows[:, HALF:]
    tail = first_rows[192:]
    planes = jnp.stack(
        [first_rows]
        + [jnp.concatenate([part, tail]) for part in (gate_rows, up_rows, down_rows)]
    )
    summed = scatter_sum(planes, "z")

    rows = summed[:192].reshape(2, 96, HALF)
    keep = lax.dynamic_index_in_dim(rows, core, 0, keepdims=False)
    send = lax.dynamic_index_in_dim(rows, 1 - core, 0, keepdims=False)
    got = swap_core(jnp.concatenate([send, summed[192:200]]))
    gain_sums = (summed[192:196] + got[96:100]).reshape(2, WIDTH)
    gain_grad = lax.dynamic_slice_in_dim(gain_sums, lax.axis_index(AXES) * 6, 6, 1)
    halves = by_core(core, keep, got[:96])
    as_columns = jnp.concatenate([halves[0], halves[1]], axis=1)
    as_down = halves.reshape(2, 2, 48, HALF).transpose(0, 2, 1, 3).reshape(96, WIDTH)
    as_out = halves.reshape(2, 2, 4, 12, HALF).transpose(2, 0, 3, 1, 4).reshape(96, WIDTH)
    unit_grad = jnp.where(z == 3, as_down, jnp.where((z == 0) & (y == 3), as_out, as_columns))

    moment_next = MOMENTUM * moment_rows + unit_grad
    line = gather_four(moment_next.astype(BF), "x")
    unit, gram_rows = gram_of(place, line, swap_core(line))
    gram_sum = gram_rows.astype(F32)
    for step in (1, 3, 2):
        pairs = [
            (4 * plane + at, 4 * plane + (at + step) % 4) for plane in (1, 2, 3) for at in range(4)
        ]
        gram_sum = gram_sum + lax.ppermute(gram_rows, ("z", "y"), pairs).astype(F32)
    gram_rows = gram_sum.astype(BF)
    line = gather_four(gram_rows, "x")
    result = polish(place, line, swap_core(line), unit)

    returned = to_owners(jnp.stack([unit_grad.astype(BF), result]), z == 3)
    sums, turned_parts = lax.optimization_barrier(
        (owned_parts(returned[0]), owned_parts(returned[1]))
    )
    moments = [
        MOMENTUM * old + new
        for old, new in zip((qkv_moment, out_moment, inner_moment, down_moment), sums)
    ]
    weights_new = [
        old * (1.0 - MUON_RATE * WEIGHT_DECAY)
        - MUON_RATE * (0.2 * math.sqrt(longest)) * turned
        for old, turned, longest in zip(
            (qkv_weight, out_weight, inner_weight, down_weight),
            turned_parts,
            (WIDTH, WIDTH, 4 * WIDTH, 4 * WIDTH),
        )
    ]
    gain_next = GAIN_MOMENTUM * gain_moment + gain_grad
    gains_new = gains - GAIN_RATE * gain_next
    return (
        block_output,
        input_grad,
        gain_grad,
        gain_next,
        gains_new,
        *sums,
        *weights_new,
        *moments,
    )


def solution(mesh):
    grid = Mesh(mesh.devices.reshape(4, 4, 4, 2), AXES)
    rows = P(AXES, None)
    middle = P(None, AXES)
    stacked = P(None, AXES, None)
    weights = (stacked, rows, stacked, rows)
    in_specs = (rows, rows, rows, middle, middle) + weights + weights
    out_specs = (rows, rows, middle, middle, middle) + weights * 3
    return jax.shard_map(
        per_device, mesh=grid, in_specs=in_specs, out_specs=out_specs, check_vma=False
    )
```

```python
import math

import jax
import jax.numpy as jnp
import numpy as np
from jax import lax
from jax.experimental import pallas as pl
from jax.sharding import Mesh
from jax.sharding import PartitionSpec as P

HEAD = 64
HALF = 384
WIDTH = 768
PACK = 128
EPSILON = 1e-06
ROPE_BASE = 10000.0
MOMENTUM = 0.95
GAIN_MOMENTUM = 0.9
MUON_RATE = 0.3
GAIN_RATE = 0.001
WEIGHT_DECAY = 0.1
POLY_LINEAR = 3.4445
POLY_CUBIC = -4.775
POLY_QUINTIC = 2.0315

AXES = ("z", "y", "x", "c")
SWAP = [(0, 1), (1, 0)]
BF = jnp.bfloat16
F32 = jnp.float32


def mm(left, right):
    return jnp.dot(left, right, preferred_element_type=F32)


def mm_nt(left, right):
    return lax.dot_general(left, right, (((1,), (1,)), ((), ())), preferred_element_type=F32)


def mm_tn(left, right):
    return lax.dot_general(left, right, (((0,), (0,)), ((), ())), preferred_element_type=F32)


def swap_core(value):
    return lax.ppermute(value, "c", SWAP)


def by_core(core, own, other):
    return jnp.where(core == 0, jnp.stack([own, other]), jnp.stack([other, own]))


def shift(axis, step):
    return [(i, (i + step) % 4) for i in range(4)]


def scatter_sum(chunks, axis):
    me = lax.axis_index(axis)
    total = lax.dynamic_index_in_dim(chunks, me, 0, keepdims=False).astype(F32)
    for step in (1, 3, 2):
        piece = lax.dynamic_index_in_dim(chunks, (me + step) % 4, 0, keepdims=False)
        total = total + lax.ppermute(piece, axis, shift(axis, step)).astype(F32)
    return total


def gather_four(value, axis):
    me = lax.axis_index(axis)
    full = jnp.zeros((4,) + value.shape, value.dtype)
    full = lax.dynamic_update_index_in_dim(full, value, me, 0)
    for step in (1, 3, 2):
        got = lax.ppermute(value, axis, shift(axis, step))
        full = lax.dynamic_update_index_in_dim(full, got, (me + 4 - step) % 4, 0)
    return full


def exchange(value, axis):
    me = lax.axis_index(axis)
    kept = lax.dynamic_index_in_dim(value, me, 0, keepdims=False)
    full = lax.dynamic_update_index_in_dim(jnp.zeros_like(value), kept, me, 0)
    for step in (1, 3, 2):
        piece = lax.dynamic_index_in_dim(value, (me + step) % 4, 0, keepdims=False)
        got = lax.ppermute(piece, axis, shift(axis, step))
        full = lax.dynamic_update_index_in_dim(full, got, (me + 4 - step) % 4, 0)
    return full


def one_hot(order):
    table = np.zeros((len(order), len(order)), np.float32)
    table[np.arange(len(order)), np.asarray(order)] = 1.0
    return jnp.asarray(table, BF)


def norm_order():
    grid = np.arange(WIDTH).reshape(4, 4, 4, 2, 6)
    return grid.transpose(2, 3, 1, 0, 4).reshape(-1)


def out_order():
    grid = np.arange(HALF).reshape(2, 4, 4, 2, 6)
    return grid.transpose(2, 3, 1, 0, 4).reshape(-1)


def down_order():
    grid = np.arange(4 * HALF).reshape(4, 2, 4, 2, 24)
    return grid.transpose(2, 0, 3, 1, 4).reshape(-1)


def segment_table(lengths, count):
    ends = jnp.cumsum(lengths, dtype=jnp.int32)
    places = jnp.arange(count, dtype=jnp.int32)
    segment = jnp.sum((places[:, None] >= ends[None, :]).astype(jnp.int32), axis=1, dtype=jnp.int32)
    starts = ends - lengths
    slots = jnp.arange(lengths.shape[0], dtype=jnp.int32)
    first = jnp.sum(
        jnp.where(segment[:, None] == slots[None, :], starts[None, :], 0), axis=1, dtype=jnp.int32
    )
    return (segment, places - first)


def norm_scale(values):
    return lax.rsqrt(jnp.mean(values * values, axis=-1, keepdims=True) + EPSILON)


def norm_backward(values, scale, gain, grad):
    scaled = grad * gain
    return scale * scaled - values * (scale * scale * scale) * jnp.mean(
        scaled * values, axis=-1, keepdims=True
    )


def to_units(qkv, out, inner, down):
    first = jnp.concatenate([qkv, out[None]])
    wide = inner.reshape(2, 6, 4, WIDTH).transpose(0, 2, 1, 3)
    pieces = jnp.concatenate([first[None], wide, down.reshape(1, 4, 6, WIDTH)])
    got = exchange(pieces, "z")
    turned = jnp.where(lax.axis_index("z") == 3, got, got.transpose(1, 0, 2, 3))
    return exchange(turned, "y").reshape(96, WIDTH)


def to_owners(rows, planes_last):
    sent = rows.reshape(2, 4, 4, 6, WIDTH).swapaxes(0, 1)
    got = exchange(sent, "y").swapaxes(0, 1)
    turned = jnp.where(planes_last, got, got.swapaxes(1, 2))
    back = exchange(turned.swapaxes(0, 1), "z").swapaxes(0, 1)
    return back.astype(F32)


def owned_parts(rows):
    inner = rows[1:3].transpose(0, 2, 1, 3).reshape(2, 6, 4 * WIDTH)
    return rows[0, :3], rows[0, 3], inner, rows[3].reshape(24, WIDTH)


def rotation_tables():
    freq = ROPE_BASE ** (-np.arange(HEAD // 2) / (HEAD // 2))
    angle = np.arange(PACK)[:, None] * freq[None, :]
    return jnp.asarray(np.cos(angle), F32), jnp.asarray(np.sin(angle), F32)


def blocks_of(grid, group, part):
    block = lax.dynamic_slice(grid, (0, group, part * 48, 0), (16, 1, 48, HALF))
    return block.reshape(WIDTH, HALF)


def tall_blocks(grid, block, core):
    tall = grid.reshape(4, 2, 8, 2, 208, HALF)
    return [
        lax.dynamic_slice(
            tall, (block, core, 0, half, 144, 0), (1, 1, 8, 1, 48, HALF)
        ).reshape(HALF, HALF)
        for half in range(2)
    ]


def heads_of(values):
    return values.reshape(2, PACK, HALF // HEAD, HEAD)


def turn_rows(order_hot, values):
    return mm_nt(order_hot, values).astype(BF)


def attend(place, tokens, gain, cosine, sine, mask, grid, turn):
    core = place[0]
    inputs = tokens.astype(F32)
    normed = (inputs * norm_scale(inputs) * gain).astype(BF)
    weights = [blocks_of(grid, 2 * index + core, 0) for index in range(3)]
    query = rotate(heads_of(mm(normed, weights[0])), cosine, sine).astype(BF)
    keys = rotate(heads_of(mm(normed, weights[1])), cosine, sine).astype(BF)
    values = heads_of(mm(normed, weights[2]).astype(BF))
    dots = jnp.einsum("pqhd,pkhd->phqk", query, keys, preferred_element_type=F32)
    dots = jnp.where(mask[:, None] > 0.0, dots * HEAD**-0.5, -1e30)
    chances = jnp.exp(dots - jnp.max(dots, axis=-1, keepdims=True))
    chances = chances / jnp.sum(chances, axis=-1, keepdims=True)
    mixed = jnp.einsum(
        "phqk,pkhd->pqhd", chances.astype(BF), values, preferred_element_type=F32
    )
    mixed = mixed.astype(BF).reshape(2 * PACK, HALF)
    return mixed, query, keys, values, chances, turn_rows(turn, normed), weights


def by_slots(values, at):
    return [lax.dynamic_index_in_dim(values, (at + step) % 4, 0, keepdims=False) for step in range(4)]


def gated(place, tokens, own_mixed, other_mixed, cot, gain, grid, turn, turn_down):
    core, x, y = place[0], place[1], place[2]
    both = by_core(core, own_mixed, other_mixed)
    mixed = jnp.concatenate([both[0], both[1]], axis=1)
    out_full = jnp.concatenate([blocks_of(grid, 6, 0), blocks_of(grid, 7, 0)], axis=1)
    middle = tokens.astype(F32) + mm(mixed, out_full)
    scale = norm_scale(middle)
    low = (middle * scale * gain).astype(BF)
    weights, parts, hiddens = [], [], []
    for slot in range(4):
        group = 2 * ((y + slot) % 4) + core
        w_gate, w_up = blocks_of(grid, group, 1), blocks_of(grid, group, 2)
        gate = mm(low, w_gate)
        upward = mm(low, w_up)
        sigma = jax.nn.sigmoid(gate)
        activated = gate * sigma
        weights.append((w_gate, w_up))
        parts.append((gate, upward, sigma, activated))
        hiddens.append((activated * upward).astype(BF))
    turned = turn_rows(turn_down, jnp.concatenate(hiddens, axis=1))
    downs = [
        mm(lax.dynamic_slice_in_dim(turned, (x + slot) % 4 * HALF, HALF, 0), cot).astype(BF)
        for slot in range(4)
    ]
    cot, downs = lax.optimization_barrier((cot, downs))
    two_part, down_part = 0.0, 0.0
    gate_grads, up_grads = [], []
    for slot in range(4):
        gate, upward, sigma, activated = parts[slot]
        w_gate, w_up = weights[slot]
        w_down = jnp.concatenate(tall_blocks(grid, (y + slot) % 4, core), axis=1)
        hidden_grad = mm_nt(cot, w_down)
        gate_grad = (hidden_grad * upward * (sigma * (1.0 + gate * (1.0 - sigma)))).astype(BF)
        up_grad = (hidden_grad * activated).astype(BF)
        two_part = two_part + (mm_nt(gate_grad, w_gate) + mm_nt(up_grad, w_up))
        down_part = down_part + mm(hiddens[slot], w_down)
        gate_grads.append(gate_grad)
        up_grads.append(up_grad)
    two_part, gate_grads, up_grads = lax.optimization_barrier((two_part, gate_grads, up_grads))
    turned = turn_rows(turn, low)
    wides = [
        mm(turned, jnp.concatenate(pair, axis=1)).astype(BF) for pair in zip(up_grads, gate_grads)
    ]
    gain_part = jnp.sum(two_part * middle * scale, axis=0, keepdims=True)
    return middle, two_part, down_part, gain_part, downs, wides


def attend_back(
    place, tokens, middle, normed_two_grad, cot, gains, gain_two, cosine, sine, grid,
    mixed, query, keys, values, probs, one_turned, turn_out, weights,
):
    core, x = place[0], place[1]
    grad = cot.astype(F32) + norm_backward(
        middle, norm_scale(middle), gains[1:2, :], normed_two_grad
    )
    branch_grad = grad.astype(BF)
    half = grid.reshape(2, 8, 8, 208, HALF)
    out_rows = [
        lax.dynamic_slice(half, (core, 0, group, 0, 0), (1, 8, 1, 48, HALF)).reshape(HALF, HALF)
        for group in (6, 7)
    ]
    mixed_grad = mm_nt(branch_grad, jnp.concatenate(out_rows, axis=1)).astype(BF)
    out_turned = turn_rows(turn_out, mixed)
    grads = heads_of(mixed_grad)
    values_grad = jnp.einsum(
        "phqk,pqhd->pkhd", probs.astype(BF), grads, preferred_element_type=F32
    )
    probs_grad = jnp.einsum("pqhd,pkhd->phqk", grads, values, preferred_element_type=F32)
    centre = jnp.sum(probs * probs_grad, axis=-1, keepdims=True)
    dots = (probs * (probs_grad - centre) * HEAD**-0.5).astype(BF)
    query_grad = jnp.einsum("phqk,pkhd->pqhd", dots, keys, preferred_element_type=F32)
    keys_grad = jnp.einsum("phqk,pqhd->pkhd", dots, query, preferred_element_type=F32)
    flat = (2 * PACK, HALF)
    low = [
        rotate(query_grad, cosine, -sine).astype(BF).reshape(flat),
        rotate(keys_grad, cosine, -sine).astype(BF).reshape(flat),
        values_grad.reshape(flat).astype(BF),
    ]
    total = sum(mm_nt(part, weight) for part, weight in zip(low, weights))
    inputs = tokens.astype(F32)
    gain_one = jnp.sum(total * inputs * norm_scale(inputs), axis=0, keepdims=True)
    tail = jnp.concatenate([gain_one, gain_two]).reshape(4, HALF)
    tail = jnp.pad(tail, ((0, 12), (0, 0))).astype(BF)
    tails = jnp.tile(tail, (1, 4))
    wide = jnp.concatenate(low, axis=1)
    slots = []
    for slot in range(4):
        at = (x + slot) % 4
        columns = mm(lax.dynamic_slice_in_dim(one_turned, at * 192, 192, 0), wide)
        rows = mm(lax.dynamic_slice_in_dim(out_turned, at * 96, 96, 0), branch_grad)
        rows = jnp.concatenate(
            [rows[48 * part : 48 * part + 48, half : half + HALF] for part in (0, 1) for half in (0, HALF)]
        )
        piece = jnp.concatenate([columns.astype(BF), rows.astype(BF)], axis=1)
        slots.append(jnp.concatenate([piece, tails]))
    return grad, total, slots


def rotate(values, cosine, sine):
    half = HEAD // 2
    first, second = values[..., :half], values[..., half:]
    return jnp.concatenate(
        [first * cosine - second * sine, second * cosine + first * sine], axis=-1
    )


def gram_of(place, own_line, other_line):
    core, x, plane = place[0], place[1], place[3]
    unit = jnp.moveaxis(by_core(core, own_line, other_line), 0, 1).reshape(WIDTH, WIDTH)
    full = jnp.where(plane == 3, mm_tn(unit, unit), mm_nt(unit, unit))
    return unit, lax.dynamic_slice_in_dim(full, (2 * x + core) * 96, 96, 0).astype(BF)


def polish(place, own_line, other_line, unit):
    core, x, plane = place[0], place[1], place[3]
    slot = 2 * x + core
    gram = jnp.moveaxis(by_core(core, own_line, other_line), 0, 1).reshape(WIDTH, WIDTH)
    at = lax.broadcasted_iota(jnp.int32, gram.shape, 0)
    diagonal = at == lax.broadcasted_iota(jnp.int32, gram.shape, 1)
    size = jnp.sqrt(jnp.sum(jnp.where(diagonal, gram.astype(F32), 0.0))) + 1e-07
    scale = 1.0 / (size * size)
    square = gram.astype(F32) * scale
    poly = POLY_CUBIC * square + POLY_QUINTIC * (mm(gram, gram) * (scale * scale))
    poly_low = poly.astype(BF)
    one = mm(gram, poly_low) * scale
    square = POLY_LINEAR**2 * square + 2.0 * POLY_LINEAR * one + mm(one.astype(BF), poly_low)
    low = square.astype(BF)
    poly_next = POLY_CUBIC * square + POLY_QUINTIC * mm(low, low)
    factor = POLY_LINEAR * (poly + poly_next) + mm(poly_next.astype(BF), poly_low)
    factor = factor.astype(BF)
    own = lax.dynamic_slice_in_dim(unit, slot * 96, 96, 0)
    left = jnp.where(plane == 3, own, lax.dynamic_slice_in_dim(factor, slot * 96, 96, 0))
    right = jnp.where(plane == 3, factor, unit)
    result = (mm(left, right) + POLY_LINEAR**2 * own.astype(F32)) / size
    return result.astype(BF)


def join_kernel(own, other, total):
    total[...] = own[...] + other[...]


def join_cores(own, other):
    return pl.pallas_call(
        join_kernel,
        out_shape=jax.ShapeDtypeStruct(own.shape, F32),
        cost_estimate=pl.CostEstimate(
            flops=5 * 10**10, bytes_accessed=3 * 10**6, transcendentals=0
        ),
        name="join_cores",
    )(own, other)


def send_slots(slots, axis):
    got = [lax.ppermute(slots[step], axis, shift(axis, step)) for step in (1, 3, 2)]
    return [slots[0]] + got


def sum_pieces(pieces):
    total = pieces[0].astype(F32)
    for piece in pieces[1:]:
        total = total + piece.astype(F32)
    return total


def sum_slots(slots, axis):
    return sum_pieces(send_slots(slots, axis))


def per_device(
    tokens,
    cotangent,
    lengths,
    gains,
    gain_moment,
    qkv_weight,
    out_weight,
    inner_weight,
    down_weight,
    qkv_moment,
    out_moment,
    inner_moment,
    down_moment,
):
    z, y, x, core = (lax.axis_index(name) for name in AXES)
    place = jnp.stack([core, x, y, z]).astype(jnp.int32)
    first = jnp.concatenate([qkv_weight, out_weight[None]]).astype(BF)
    first = first.reshape(4, 6, 2, HALF).transpose(0, 2, 1, 3)
    wide = inner_weight.astype(BF).reshape(2, 6, 4, 2, HALF).transpose(0, 2, 3, 1, 4)
    blocks = jnp.stack([first, wide[0], wide[1]], axis=2).reshape(8, 3, 6, HALF)
    blocks = lax.all_to_all(blocks, ("x", "c"), split_axis=0, concat_axis=0, tiled=True)
    blocks = blocks.transpose(1, 0, 2, 3).reshape(144, HALF)
    down_low = down_weight.astype(BF)
    down_keep = jnp.where(core == 0, down_low[:, :HALF], down_low[:, HALF:])
    down_send = jnp.where(core == 0, down_low[:, HALF:], down_low[:, :HALF])
    down_piece = by_core(core, down_keep, swap_core(down_send)).reshape(48, HALF)
    gain_piece = lax.dynamic_update_slice_in_dim(
        jnp.zeros((2, WIDTH), F32), gains, lax.axis_index(AXES) * 6, 1
    )
    gain_piece = jnp.pad(gain_piece.reshape(4, HALF), ((0, 12), (0, 0))).astype(BF)
    piece = jnp.concatenate([blocks, down_piece, gain_piece])
    whole = lax.all_gather(piece, AXES, axis=0, tiled=True)
    tokens2 = by_core(core, tokens, swap_core(tokens)).reshape(2 * PACK, WIDTH)
    cot2 = by_core(core, cotangent, swap_core(cotangent)).reshape(2 * PACK, WIDTH)
    lengths2 = by_core(core, lengths[0], swap_core(lengths[0].astype(F32)).astype(jnp.int32))
    moment_rows = to_units(qkv_moment, out_moment, inner_moment, down_moment)
    segment, position = jax.vmap(lambda row: segment_table(row, PACK))(lengths2)
    tables = rotation_tables()
    cosine, sine = (table[position][:, :, None, :] for table in tables)
    places = jnp.arange(PACK, dtype=jnp.int32)
    allowed = (segment[:, :, None] == segment[:, None, :]) & (places[None, :] <= places[:, None])
    mask = allowed.astype(F32)
    turn, turn_out, turn_down = (
        one_hot(order()) for order in (norm_order, out_order, down_order)
    )
    whole, moment_rows, tokens2, cot2, cosine, sine, mask = lax.optimization_barrier(
        (whole, moment_rows, tokens2, cot2, cosine, sine, mask)
    )

    grid = whole.reshape(16, 8, 208, HALF)
    gains_full = jnp.sum(grid[:, :, 192:196].astype(F32), axis=(0, 1)).reshape(2, WIDTH)
    mixed, query, keys, values, probs, one_turned, weights = attend(
        place, tokens2, gains_full[0:1], cosine, sine, mask, grid, turn
    )
    results = gated(
        place, tokens2, mixed, swap_core(mixed), cot2, gains_full[1:2], grid, turn, turn_down
    )
    middle, two_part, down_part, gain_two, down_slots, wide_slots = results
    two_other = swap_core(two_part)
    down_pieces = send_slots(down_slots, "x")
    wide_pieces = send_slots(wide_slots, "y")
    normed_two_grad = join_cores(two_part, two_other)

    def own_pack(value):
        return lax.dynamic_slice_in_dim(value, core * PACK, PACK, 0)

    def other_pack(value):
        return lax.dynamic_slice_in_dim(value, (1 - core) * PACK, PACK, 0)

    results = attend_back(
        place, tokens2, middle, normed_two_grad, cot2, gains_full, gain_two, cosine, sine,
        grid, mixed, query, keys, values, probs, one_turned, turn_out, weights,
    )
    middle_grad, one_part, first_slots = results
    first_pieces = send_slots(first_slots, "x")
    _, down_pieces, wide_pieces = lax.optimization_barrier(
        (first_slots[0], down_pieces, wide_pieces)
    )
    down_rows = sum_pieces(down_pieces).astype(BF)
    wide_rows = sum_pieces(wide_pieces).astype(BF)
    first_rows = sum_pieces(first_pieces).astype(BF)

    block_output = (
        own_pack(middle) + own_pack(down_part) + swap_core(other_pack(down_part))
    ).astype(BF)
    normed_grad = own_pack(one_part) + swap_core(other_pack(one_part))
    own_inputs = tokens.astype(F32)
    input_grad = own_pack(middle_grad) + norm_backward(
        own_inputs, norm_scale(own_inputs), gains_full[0], normed_grad
    )

    wide_rows = scatter_sum(wide_rows.reshape(4, 192, WIDTH), "x").astype(BF)
    line_slots = []
    for at in range(4):
        first = lax.dynamic_slice_in_dim(first_rows, (y + at) % 4 * HALF, HALF, 1)
        down = down_rows[96 * at : 96 * at + 96]
        line_slots.append(jnp.concatenate([first, down[:, :HALF], down[:, HALF:]]))
    line_rows = sum_slots(line_slots, "y").astype(BF)
    first_rows, down_rows = line_rows[:208], line_rows[208:].reshape(2, 2, 48, HALF)
    down_rows = down_rows.transpose(1, 0, 2, 3).reshape(192, HALF)
    up_rows, gate_rows = wide_rows[:, :HALF], wide_rows[:, HALF:]
    tail = first_rows[192:]
    planes = jnp.stack(
        [first_rows]
        + [jnp.concatenate([part, tail]) for part in (gate_rows, up_rows, down_rows)]
    )
    summed = scatter_sum(planes, "z")

    rows = summed[:192].reshape(2, 96, HALF)
    keep = lax.dynamic_index_in_dim(rows, core, 0, keepdims=False)
    send = lax.dynamic_index_in_dim(rows, 1 - core, 0, keepdims=False)
    got = swap_core(jnp.concatenate([send, summed[192:200]]))
    gain_sums = (summed[192:196] + got[96:100]).reshape(2, WIDTH)
    gain_grad = lax.dynamic_slice_in_dim(gain_sums, lax.axis_index(AXES) * 6, 6, 1)
    halves = by_core(core, keep, got[:96])
    as_columns = jnp.concatenate([halves[0], halves[1]], axis=1)
    as_down = halves.reshape(2, 2, 48, HALF).transpose(0, 2, 1, 3).reshape(96, WIDTH)
    as_out = halves.reshape(2, 2, 4, 12, HALF).transpose(2, 0, 3, 1, 4).reshape(96, WIDTH)
    unit_grad = jnp.where(z == 3, as_down, jnp.where((z == 0) & (y == 3), as_out, as_columns))

    moment_next = MOMENTUM * moment_rows + unit_grad
    line = gather_four(moment_next.astype(BF), "x")
    unit, gram_rows = gram_of(place, line, swap_core(line))
    gram_sum = gram_rows.astype(F32)
    for step in (1, 3, 2):
        pairs = [
            (4 * plane + at, 4 * plane + (at + step) % 4) for plane in (1, 2, 3) for at in range(4)
        ]
        gram_sum = gram_sum + lax.ppermute(gram_rows, ("z", "y"), pairs).astype(F32)
    gram_rows = gram_sum.astype(BF)
    line = gather_four(gram_rows, "x")
    result = polish(place, line, swap_core(line), unit)

    returned = to_owners(jnp.stack([unit_grad.astype(BF), result]), z == 3)
    sums, turned_parts = lax.optimization_barrier(
        (owned_parts(returned[0]), owned_parts(returned[1]))
    )
    moments = [
        MOMENTUM * old + new
        for old, new in zip((qkv_moment, out_moment, inner_moment, down_moment), sums)
    ]
    weights_new = [
        old * (1.0 - MUON_RATE * WEIGHT_DECAY)
        - MUON_RATE * (0.2 * math.sqrt(longest)) * turned
        for old, turned, longest in zip(
            (qkv_weight, out_weight, inner_weight, down_weight),
            turned_parts,
            (WIDTH, WIDTH, 4 * WIDTH, 4 * WIDTH),
        )
    ]
    gain_next = GAIN_MOMENTUM * gain_moment + gain_grad
    gains_new = gains - GAIN_RATE * gain_next
    return (
        block_output,
        input_grad,
        gain_grad,
        gain_next,
        gains_new,
        *sums,
        *weights_new,
        *moments,
    )


def solution(mesh):
    grid = Mesh(mesh.devices.reshape(4, 4, 4, 2), AXES)
    rows = P(AXES, None)
    middle = P(None, AXES)
    stacked = P(None, AXES, None)
    weights = (stacked, rows, stacked, rows)
    in_specs = (rows, rows, rows, middle, middle) + weights + weights
    out_specs = (rows, rows, middle, middle, middle) + weights * 3
    return jax.shard_map(
        per_device, mesh=grid, in_specs=in_specs, out_specs=out_specs, check_vma=False
    )
```

```python
import math

import jax
import jax.numpy as jnp
import numpy as np
from jax import lax
from jax.sharding import Mesh
from jax.sharding import PartitionSpec as P

HEAD = 64
HALF = 384
WIDTH = 768
PACK = 128
EPSILON = 1e-06
ROPE_BASE = 10000.0
MOMENTUM = 0.95
GAIN_MOMENTUM = 0.9
MUON_RATE = 0.3
GAIN_RATE = 0.001
WEIGHT_DECAY = 0.1
POLY_LINEAR = 3.4445
POLY_CUBIC = -4.775
POLY_QUINTIC = 2.0315

AXES = ("z", "y", "x", "c")
SWAP = [(0, 1), (1, 0)]
BF = jnp.bfloat16
F32 = jnp.float32


def mm(left, right):
    return jnp.dot(left, right, preferred_element_type=F32)


def mm_nt(left, right):
    return lax.dot_general(left, right, (((1,), (1,)), ((), ())), preferred_element_type=F32)


def mm_tn(left, right):
    return lax.dot_general(left, right, (((0,), (0,)), ((), ())), preferred_element_type=F32)


def swap_core(value):
    return lax.ppermute(value, "c", SWAP)


def by_core(core, own, other):
    return jnp.where(core == 0, jnp.stack([own, other]), jnp.stack([other, own]))


def shift(axis, step):
    return [(i, (i + step) % 4) for i in range(4)]


def scatter_sum(chunks, axis):
    me = lax.axis_index(axis)
    total = lax.dynamic_index_in_dim(chunks, me, 0, keepdims=False).astype(F32)
    for step in (1, 3, 2):
        piece = lax.dynamic_index_in_dim(chunks, (me + step) % 4, 0, keepdims=False)
        total = total + lax.ppermute(piece, axis, shift(axis, step)).astype(F32)
    return total


def gather_four(value, axis):
    me = lax.axis_index(axis)
    full = jnp.zeros((4,) + value.shape, value.dtype)
    full = lax.dynamic_update_index_in_dim(full, value, me, 0)
    for step in (1, 3, 2):
        got = lax.ppermute(value, axis, shift(axis, step))
        full = lax.dynamic_update_index_in_dim(full, got, (me + 4 - step) % 4, 0)
    return full


def exchange(value, axis):
    me = lax.axis_index(axis)
    kept = lax.dynamic_index_in_dim(value, me, 0, keepdims=False)
    full = lax.dynamic_update_index_in_dim(jnp.zeros_like(value), kept, me, 0)
    for step in (1, 3, 2):
        piece = lax.dynamic_index_in_dim(value, (me + step) % 4, 0, keepdims=False)
        got = lax.ppermute(piece, axis, shift(axis, step))
        full = lax.dynamic_update_index_in_dim(full, got, (me + 4 - step) % 4, 0)
    return full


def one_hot(order):
    table = np.zeros((len(order), len(order)), np.float32)
    table[np.arange(len(order)), np.asarray(order)] = 1.0
    return jnp.asarray(table, BF)


def norm_order():
    grid = np.arange(WIDTH).reshape(4, 4, 4, 2, 6)
    return grid.transpose(2, 3, 1, 0, 4).reshape(-1)


def out_order():
    grid = np.arange(HALF).reshape(2, 4, 4, 2, 6)
    return grid.transpose(2, 3, 1, 0, 4).reshape(-1)


def down_order():
    grid = np.arange(4 * HALF).reshape(4, 2, 4, 2, 24)
    return grid.transpose(2, 0, 3, 1, 4).reshape(-1)


def segment_table(lengths, count):
    ends = jnp.cumsum(lengths, dtype=jnp.int32)
    places = jnp.arange(count, dtype=jnp.int32)
    segment = jnp.sum((places[:, None] >= ends[None, :]).astype(jnp.int32), axis=1, dtype=jnp.int32)
    starts = ends - lengths
    slots = jnp.arange(lengths.shape[0], dtype=jnp.int32)
    first = jnp.sum(
        jnp.where(segment[:, None] == slots[None, :], starts[None, :], 0), axis=1, dtype=jnp.int32
    )
    return (segment, places - first)


def norm_scale(values):
    return lax.rsqrt(jnp.mean(values * values, axis=-1, keepdims=True) + EPSILON)


def norm_backward(values, scale, gain, grad):
    scaled = grad * gain
    return scale * scaled - values * (scale * scale * scale) * jnp.mean(
        scaled * values, axis=-1, keepdims=True
    )


def to_units(qkv, out, inner, down):
    first = jnp.concatenate([qkv, out[None]])
    wide = inner.reshape(2, 6, 4, WIDTH).transpose(0, 2, 1, 3)
    pieces = jnp.concatenate([first[None], wide, down.reshape(1, 4, 6, WIDTH)])
    got = exchange(pieces, "z")
    turned = jnp.where(lax.axis_index("z") == 3, got, got.transpose(1, 0, 2, 3))
    return exchange(turned, "y").reshape(96, WIDTH)


def to_owners(rows, planes_last):
    sent = rows.reshape(2, 4, 4, 6, WIDTH).swapaxes(0, 1)
    got = exchange(sent, "y").swapaxes(0, 1)
    turned = jnp.where(planes_last, got, got.swapaxes(1, 2))
    back = exchange(turned.swapaxes(0, 1), "z").swapaxes(0, 1)
    return back.astype(F32)


def owned_parts(rows):
    inner = rows[1:3].transpose(0, 2, 1, 3).reshape(2, 6, 4 * WIDTH)
    return rows[0, :3], rows[0, 3], inner, rows[3].reshape(24, WIDTH)


def rotation_tables():
    freq = ROPE_BASE ** (-np.arange(HEAD // 2) / (HEAD // 2))
    angle = np.arange(PACK)[:, None] * freq[None, :]
    return jnp.asarray(np.cos(angle), F32), jnp.asarray(np.sin(angle), F32)


def blocks_of(grid, group, part):
    block = lax.dynamic_slice(grid, (0, group, part * 48, 0), (16, 1, 48, HALF))
    return block.reshape(WIDTH, HALF)


def tall_blocks(grid, block, core):
    tall = grid.reshape(4, 2, 8, 2, 208, HALF)
    return [
        lax.dynamic_slice(
            tall, (block, core, 0, half, 144, 0), (1, 1, 8, 1, 48, HALF)
        ).reshape(HALF, HALF)
        for half in range(2)
    ]


def heads_of(values):
    return values.reshape(2, PACK, HALF // HEAD, HEAD)


def turn_rows(order_hot, values):
    return mm_nt(order_hot, values).astype(BF)


def attend(place, tokens, gain, cosine, sine, mask, grid, turn):
    core = place[0]
    inputs = tokens.astype(F32)
    normed = (inputs * norm_scale(inputs) * gain).astype(BF)
    weights = [blocks_of(grid, 2 * index + core, 0) for index in range(3)]
    query = rotate(heads_of(mm(normed, weights[0])), cosine, sine).astype(BF)
    keys = rotate(heads_of(mm(normed, weights[1])), cosine, sine).astype(BF)
    values = heads_of(mm(normed, weights[2]).astype(BF))
    dots = jnp.einsum("pqhd,pkhd->phqk", query, keys, preferred_element_type=F32)
    dots = jnp.where(mask[:, None] > 0.0, dots * HEAD**-0.5, -1e30)
    chances = jnp.exp(dots - jnp.max(dots, axis=-1, keepdims=True))
    chances = chances / jnp.sum(chances, axis=-1, keepdims=True)
    mixed = jnp.einsum(
        "phqk,pkhd->pqhd", chances.astype(BF), values, preferred_element_type=F32
    )
    mixed = mixed.astype(BF).reshape(2 * PACK, HALF)
    return mixed, query, keys, values, chances, turn_rows(turn, normed), weights


def by_slots(values, at):
    return [lax.dynamic_index_in_dim(values, (at + step) % 4, 0, keepdims=False) for step in range(4)]


def gated(place, tokens, own_mixed, other_mixed, cot, gain, grid, turn, turn_down):
    core, x, y = place[0], place[1], place[2]
    both = by_core(core, own_mixed, other_mixed)
    mixed = jnp.concatenate([both[0], both[1]], axis=1)
    out_full = jnp.concatenate([blocks_of(grid, 6, 0), blocks_of(grid, 7, 0)], axis=1)
    middle = tokens.astype(F32) + mm(mixed, out_full)
    scale = norm_scale(middle)
    low = (middle * scale * gain).astype(BF)
    weights, parts, hiddens = [], [], []
    for slot in range(4):
        group = 2 * ((y + slot) % 4) + core
        w_gate, w_up = blocks_of(grid, group, 1), blocks_of(grid, group, 2)
        gate = mm(low, w_gate)
        upward = mm(low, w_up)
        sigma = jax.nn.sigmoid(gate)
        activated = gate * sigma
        weights.append((w_gate, w_up))
        parts.append((gate, upward, sigma, activated))
        hiddens.append((activated * upward).astype(BF))
    turned = turn_rows(turn_down, jnp.concatenate(hiddens, axis=1))
    downs = [
        mm(lax.dynamic_slice_in_dim(turned, (x + slot) % 4 * HALF, HALF, 0), cot).astype(BF)
        for slot in range(4)
    ]
    cot, downs = lax.optimization_barrier((cot, downs))
    two_part, down_part = 0.0, 0.0
    gate_grads, up_grads = [], []
    for slot in range(4):
        gate, upward, sigma, activated = parts[slot]
        w_gate, w_up = weights[slot]
        w_down = jnp.concatenate(tall_blocks(grid, (y + slot) % 4, core), axis=1)
        hidden_grad = mm_nt(cot, w_down)
        gate_grad = (hidden_grad * upward * (sigma * (1.0 + gate * (1.0 - sigma)))).astype(BF)
        up_grad = (hidden_grad * activated).astype(BF)
        two_part = two_part + (mm_nt(gate_grad, w_gate) + mm_nt(up_grad, w_up))
        down_part = down_part + mm(hiddens[slot], w_down)
        gate_grads.append(gate_grad)
        up_grads.append(up_grad)
    two_part, gate_grads, up_grads = lax.optimization_barrier((two_part, gate_grads, up_grads))
    turned = turn_rows(turn, low)
    wides = [
        mm(turned, jnp.concatenate(pair, axis=1)).astype(BF) for pair in zip(up_grads, gate_grads)
    ]
    gain_part = jnp.sum(two_part * middle * scale, axis=0, keepdims=True)
    return middle, two_part, down_part, gain_part, downs, wides


def attend_back(
    place, tokens, middle, normed_two_grad, cot, gains, gain_two, cosine, sine, grid,
    mixed, query, keys, values, probs, one_turned, turn_out, weights,
):
    core, x = place[0], place[1]
    grad = cot.astype(F32) + norm_backward(
        middle, norm_scale(middle), gains[1:2, :], normed_two_grad
    )
    branch_grad = grad.astype(BF)
    half = grid.reshape(2, 8, 8, 208, HALF)
    out_rows = [
        lax.dynamic_slice(half, (core, 0, group, 0, 0), (1, 8, 1, 48, HALF)).reshape(HALF, HALF)
        for group in (6, 7)
    ]
    mixed_grad = mm_nt(branch_grad, jnp.concatenate(out_rows, axis=1)).astype(BF)
    out_turned = turn_rows(turn_out, mixed)
    grads = heads_of(mixed_grad)
    values_grad = jnp.einsum(
        "phqk,pqhd->pkhd", probs.astype(BF), grads, preferred_element_type=F32
    )
    probs_grad = jnp.einsum("pqhd,pkhd->phqk", grads, values, preferred_element_type=F32)
    centre = jnp.sum(probs * probs_grad, axis=-1, keepdims=True)
    dots = (probs * (probs_grad - centre) * HEAD**-0.5).astype(BF)
    query_grad = jnp.einsum("phqk,pkhd->pqhd", dots, keys, preferred_element_type=F32)
    keys_grad = jnp.einsum("phqk,pqhd->pkhd", dots, query, preferred_element_type=F32)
    flat = (2 * PACK, HALF)
    low = [
        rotate(query_grad, cosine, -sine).astype(BF).reshape(flat),
        rotate(keys_grad, cosine, -sine).astype(BF).reshape(flat),
        values_grad.reshape(flat).astype(BF),
    ]
    total = sum(mm_nt(part, weight) for part, weight in zip(low, weights))
    inputs = tokens.astype(F32)
    gain_one = jnp.sum(total * inputs * norm_scale(inputs), axis=0, keepdims=True)
    tail = jnp.concatenate([gain_one, gain_two]).reshape(4, HALF)
    tail = jnp.pad(tail, ((0, 12), (0, 0))).astype(BF)
    tails = jnp.tile(tail, (1, 4))
    wide = jnp.concatenate(low, axis=1)
    slots = []
    for slot in range(4):
        at = (x + slot) % 4
        columns = mm(lax.dynamic_slice_in_dim(one_turned, at * 192, 192, 0), wide)
        rows = mm(lax.dynamic_slice_in_dim(out_turned, at * 96, 96, 0), branch_grad)
        rows = jnp.concatenate(
            [rows[48 * part : 48 * part + 48, half : half + HALF] for part in (0, 1) for half in (0, HALF)]
        )
        piece = jnp.concatenate([columns.astype(BF), rows.astype(BF)], axis=1)
        slots.append(jnp.concatenate([piece, tails]))
    return grad, total, slots


def rotate(values, cosine, sine):
    half = HEAD // 2
    first, second = values[..., :half], values[..., half:]
    return jnp.concatenate(
        [first * cosine - second * sine, second * cosine + first * sine], axis=-1
    )


def gram_of(place, own_line, other_line):
    core, x, plane = place[0], place[1], place[3]
    unit = jnp.moveaxis(by_core(core, own_line, other_line), 0, 1).reshape(WIDTH, WIDTH)
    full = jnp.where(plane == 3, mm_tn(unit, unit), mm_nt(unit, unit))
    return unit, lax.dynamic_slice_in_dim(full, (2 * x + core) * 96, 96, 0).astype(BF)


def polish(place, own_line, other_line, unit):
    core, x, plane = place[0], place[1], place[3]
    slot = 2 * x + core
    gram = jnp.moveaxis(by_core(core, own_line, other_line), 0, 1).reshape(WIDTH, WIDTH)
    at = lax.broadcasted_iota(jnp.int32, gram.shape, 0)
    diagonal = at == lax.broadcasted_iota(jnp.int32, gram.shape, 1)
    size = jnp.sqrt(jnp.sum(jnp.where(diagonal, gram.astype(F32), 0.0))) + 1e-07
    scale = 1.0 / (size * size)
    square = gram.astype(F32) * scale
    poly = POLY_CUBIC * square + POLY_QUINTIC * (mm(gram, gram) * (scale * scale))
    poly_low = poly.astype(BF)
    one = mm(gram, poly_low) * scale
    square = POLY_LINEAR**2 * square + 2.0 * POLY_LINEAR * one + mm(one.astype(BF), poly_low)
    low = square.astype(BF)
    poly_next = POLY_CUBIC * square + POLY_QUINTIC * mm(low, low)
    factor = POLY_LINEAR * (poly + poly_next) + mm(poly_next.astype(BF), poly_low)
    factor = factor.astype(BF)
    own = lax.dynamic_slice_in_dim(unit, slot * 96, 96, 0)
    left = jnp.where(plane == 3, own, lax.dynamic_slice_in_dim(factor, slot * 96, 96, 0))
    right = jnp.where(plane == 3, factor, unit)
    result = (mm(left, right) + POLY_LINEAR**2 * own.astype(F32)) / size
    return result.astype(BF)


def send_slots(slots, axis):
    got = [lax.ppermute(slots[step], axis, shift(axis, step)) for step in (1, 3, 2)]
    return [slots[0]] + got


def sum_pieces(pieces):
    total = pieces[0].astype(F32)
    for piece in pieces[1:]:
        total = total + piece.astype(F32)
    return total


def sum_slots(slots, axis):
    return sum_pieces(send_slots(slots, axis))


def per_device(
    tokens,
    cotangent,
    lengths,
    gains,
    gain_moment,
    qkv_weight,
    out_weight,
    inner_weight,
    down_weight,
    qkv_moment,
    out_moment,
    inner_moment,
    down_moment,
):
    z, y, x, core = (lax.axis_index(name) for name in AXES)
    place = jnp.stack([core, x, y, z]).astype(jnp.int32)
    first = jnp.concatenate([qkv_weight, out_weight[None]]).astype(BF)
    first = first.reshape(4, 6, 2, HALF).transpose(0, 2, 1, 3)
    wide = inner_weight.astype(BF).reshape(2, 6, 4, 2, HALF).transpose(0, 2, 3, 1, 4)
    blocks = jnp.stack([first, wide[0], wide[1]], axis=2).reshape(8, 3, 6, HALF)
    blocks = lax.all_to_all(blocks, ("x", "c"), split_axis=0, concat_axis=0, tiled=True)
    blocks = blocks.transpose(1, 0, 2, 3).reshape(144, HALF)
    down_low = down_weight.astype(BF)
    down_keep = jnp.where(core == 0, down_low[:, :HALF], down_low[:, HALF:])
    down_send = jnp.where(core == 0, down_low[:, HALF:], down_low[:, :HALF])
    down_piece = by_core(core, down_keep, swap_core(down_send)).reshape(48, HALF)
    gain_piece = lax.dynamic_update_slice_in_dim(
        jnp.zeros((2, WIDTH), F32), gains, lax.axis_index(AXES) * 6, 1
    )
    gain_piece = jnp.pad(gain_piece.reshape(4, HALF), ((0, 12), (0, 0))).astype(BF)
    piece = jnp.concatenate([blocks, down_piece, gain_piece])
    whole = lax.all_gather(piece, AXES, axis=0, tiled=True)
    tokens2 = by_core(core, tokens, swap_core(tokens)).reshape(2 * PACK, WIDTH)
    cot2 = by_core(core, cotangent, swap_core(cotangent)).reshape(2 * PACK, WIDTH)
    lengths2 = by_core(core, lengths[0], swap_core(lengths[0].astype(F32)).astype(jnp.int32))
    moment_rows = to_units(qkv_moment, out_moment, inner_moment, down_moment)
    segment, position = jax.vmap(lambda row: segment_table(row, PACK))(lengths2)
    tables = rotation_tables()
    cosine, sine = (table[position][:, :, None, :] for table in tables)
    places = jnp.arange(PACK, dtype=jnp.int32)
    allowed = (segment[:, :, None] == segment[:, None, :]) & (places[None, :] <= places[:, None])
    mask = allowed.astype(F32)
    turn, turn_out, turn_down = (
        one_hot(order()) for order in (norm_order, out_order, down_order)
    )
    whole, moment_rows, tokens2, cot2, cosine, sine, mask = lax.optimization_barrier(
        (whole, moment_rows, tokens2, cot2, cosine, sine, mask)
    )

    grid = whole.reshape(16, 8, 208, HALF)
    gains_full = jnp.sum(grid[:, :, 192:196].astype(F32), axis=(0, 1)).reshape(2, WIDTH)
    mixed, query, keys, values, probs, one_turned, weights = attend(
        place, tokens2, gains_full[0:1], cosine, sine, mask, grid, turn
    )
    results = gated(
        place, tokens2, mixed, swap_core(mixed), cot2, gains_full[1:2], grid, turn, turn_down
    )
    middle, two_part, down_part, gain_two, down_slots, wide_slots = results
    two_other = swap_core(two_part)
    down_pieces = send_slots(down_slots, "x")
    wide_pieces = send_slots(wide_slots, "y")
    normed_two_grad = two_part + two_other

    def own_pack(value):
        return lax.dynamic_slice_in_dim(value, core * PACK, PACK, 0)

    def other_pack(value):
        return lax.dynamic_slice_in_dim(value, (1 - core) * PACK, PACK, 0)

    results = attend_back(
        place, tokens2, middle, normed_two_grad, cot2, gains_full, gain_two, cosine, sine,
        grid, mixed, query, keys, values, probs, one_turned, turn_out, weights,
    )
    middle_grad, one_part, first_slots = results
    first_pieces = send_slots(first_slots, "x")
    _, down_pieces, wide_pieces = lax.optimization_barrier(
        (first_slots[0], down_pieces, wide_pieces)
    )
    down_rows = sum_pieces(down_pieces).astype(BF)
    wide_rows = sum_pieces(wide_pieces).astype(BF)
    first_rows = sum_pieces(first_pieces).astype(BF)

    block_output = (
        own_pack(middle) + own_pack(down_part) + swap_core(other_pack(down_part))
    ).astype(BF)
    normed_grad = own_pack(one_part) + swap_core(other_pack(one_part))
    own_inputs = tokens.astype(F32)
    input_grad = own_pack(middle_grad) + norm_backward(
        own_inputs, norm_scale(own_inputs), gains_full[0], normed_grad
    )

    wide_rows = scatter_sum(wide_rows.reshape(4, 192, WIDTH), "x").astype(BF)
    line_slots = []
    for at in range(4):
        first = lax.dynamic_slice_in_dim(first_rows, (y + at) % 4 * HALF, HALF, 1)
        down = down_rows[96 * at : 96 * at + 96]
        line_slots.append(jnp.concatenate([first, down[:, :HALF], down[:, HALF:]]))
    line_rows = sum_slots(line_slots, "y").astype(BF)
    first_rows, down_rows = line_rows[:208], line_rows[208:].reshape(2, 2, 48, HALF)
    down_rows = down_rows.transpose(1, 0, 2, 3).reshape(192, HALF)
    up_rows, gate_rows = wide_rows[:, :HALF], wide_rows[:, HALF:]
    tail = first_rows[192:]
    planes = jnp.stack(
        [first_rows]
        + [jnp.concatenate([part, tail]) for part in (gate_rows, up_rows, down_rows)]
    )
    summed = scatter_sum(planes, "z")

    rows = summed[:192].reshape(2, 96, HALF)
    keep = lax.dynamic_index_in_dim(rows, core, 0, keepdims=False)
    send = lax.dynamic_index_in_dim(rows, 1 - core, 0, keepdims=False)
    got = swap_core(jnp.concatenate([send, summed[192:200]]))
    gain_sums = (summed[192:196] + got[96:100]).reshape(2, WIDTH)
    gain_grad = lax.dynamic_slice_in_dim(gain_sums, lax.axis_index(AXES) * 6, 6, 1)
    halves = by_core(core, keep, got[:96])
    as_columns = jnp.concatenate([halves[0], halves[1]], axis=1)
    as_down = halves.reshape(2, 2, 48, HALF).transpose(0, 2, 1, 3).reshape(96, WIDTH)
    as_out = halves.reshape(2, 2, 4, 12, HALF).transpose(2, 0, 3, 1, 4).reshape(96, WIDTH)
    unit_grad = jnp.where(z == 3, as_down, jnp.where((z == 0) & (y == 3), as_out, as_columns))

    moment_next = MOMENTUM * moment_rows + unit_grad
    line = gather_four(moment_next.astype(BF), "x")
    unit, gram_rows = gram_of(place, line, swap_core(line))
    gram_sum = gram_rows.astype(F32)
    for step in (1, 3, 2):
        pairs = [
            (4 * plane + at, 4 * plane + (at + step) % 4) for plane in (1, 2, 3) for at in range(4)
        ]
        gram_sum = gram_sum + lax.ppermute(gram_rows, ("z", "y"), pairs).astype(F32)
    gram_rows = gram_sum.astype(BF)
    line = gather_four(gram_rows, "x")
    result = polish(place, line, swap_core(line), unit)

    returned = to_owners(jnp.stack([unit_grad.astype(BF), result]), z == 3)
    sums, turned_parts = lax.optimization_barrier(
        (owned_parts(returned[0]), owned_parts(returned[1]))
    )
    moments = [
        MOMENTUM * old + new
        for old, new in zip((qkv_moment, out_moment, inner_moment, down_moment), sums)
    ]
    weights_new = [
        old * (1.0 - MUON_RATE * WEIGHT_DECAY)
        - MUON_RATE * (0.2 * math.sqrt(longest)) * turned
        for old, turned, longest in zip(
            (qkv_weight, out_weight, inner_weight, down_weight),
            turned_parts,
            (WIDTH, WIDTH, 4 * WIDTH, 4 * WIDTH),
        )
    ]
    gain_next = GAIN_MOMENTUM * gain_moment + gain_grad
    gains_new = gains - GAIN_RATE * gain_next
    return (
        block_output,
        input_grad,
        gain_grad,
        gain_next,
        gains_new,
        *sums,
        *weights_new,
        *moments,
    )


def solution(mesh):
    grid = Mesh(mesh.devices.reshape(4, 4, 4, 2), AXES)
    rows = P(AXES, None)
    middle = P(None, AXES)
    stacked = P(None, AXES, None)
    weights = (stacked, rows, stacked, rows)
    in_specs = (rows, rows, rows, middle, middle) + weights + weights
    out_specs = (rows, rows, middle, middle, middle) + weights * 3
    return jax.shard_map(
        per_device, mesh=grid, in_specs=in_specs, out_specs=out_specs, check_vma=False
    )
```
